256 devices in a mesh: pb: 64 (over x, z, core), ka: 4 (over y).
Axes of the slice: x: 4, y: 4, z: 8, core: 2. Of those that a mesh axis runs over, the one named last changes fastest.
Arguments:
- query_features: bfloat16 [40960, 256], P('pb', 'ka'), may hold values from -6 to 6
- key_features: bfloat16 [32768, 256], P(('ka', 'pb')), may hold values from -6 to 6
- patch_weight: bfloat16 [64, 64], replicated, may hold values from -0.75 to 0.75
- patch_bias: float32 [64], replicated, may hold values from -4 to 4
- norm_gain: float32 [64], replicated, may hold values from 0.1 to 1.9
- latent_queries: float32 [8, 128], replicated, may hold values from -240 to 240
- key_weight: bfloat16 [64, 128], replicated, may hold values from -0.75 to 0.75
- value_weight: bfloat16 [64, 128], replicated, may hold values from -0.75 to 0.75
- keep_mask: int32 [40960, 512], P('pb', 'ka'), may hold values 0 or 1
Outputs:
- latent_tokens: bfloat16 [40960, 8, 128], P('pb', 'ka')
The draws below stay inside these ranges and needn't reach their ends.
All inputs are finite; a program needn't handle non-finite values. No bound on the sum of `keep_mask` on one device may be relied on, other than what follows from the above.
Results may differ from the reference program's by a relative error of at most 0.012.
The reference program's roundings to bfloat16 on the way count: a program that leaves them out, or rounds other values in their place, can miss the bound.
Values may be sent and summed in bfloat16 or wider, within the bound.
A program may use at most 64 MiB of HBM per device.

```python
import math
import jax
import jax.numpy as jnp
from jax import lax

C = 256
E = 64
LD = 128
LAT = 8
PP = 64
KEYS = 32768
PATCHES = 512
Q = 40960


def draw_latent_queries(key, part):
    key = jax.random.fold_in(key, 11)
    base = jnp.clip(jax.random.normal(key, (LAT, LD), jnp.float32), -4.0, 4.0)
    return base


def place_ends(entries, rng, least, top_value):
    place = [jax.random.randint(jax.random.fold_in(rng, axis), (), 0, length) for axis, length in enumerate(entries.shape)]
    widest = entries.shape.index(max(entries.shape))
    next_to = place[:widest] + [(place[widest] + 1) % entries.shape[widest]] + place[widest + 1:]
    return entries.at[tuple(place)].set(least).at[tuple(next_to)].set(top_value)


def level_of(own_key, extent, cuts, least, largest):
    def one(position, blocks):
        draws = jax.random.uniform(jax.random.fold_in(jax.random.fold_in(own_key, 6), position), (blocks,), jnp.float32, least / len(cuts), largest / len(cuts))
        return jnp.repeat(jnp.exp(draws), extent[position] // blocks).reshape((-1,) + (1,) * (len(extent) - position - 1))

    level = one(*cuts[0])
    for cut in cuts[1:]:
        level = level * one(*cut)
    return level


def scatter_about(own_key, shape, deviation, limit, cuts=(), held_as=jnp.bfloat16):
    gain = level_of(own_key, shape, cuts, -0.22, 0.18) if cuts else 1.0
    drawn = jax.random.normal(own_key, shape, jnp.float32) * deviation * gain
    return jnp.minimum(jnp.maximum(drawn, -limit), limit).astype(held_as)


def setup_inputs(seed: int = 0) -> dict:
    arg_keys = jax.random.split(jax.random.key(seed), 10)
    return {
        "query_features": scatter_about(arg_keys[0], (Q, C), 1.0, 6.0, ((0, 64), (1, 4))),
        "key_features": scatter_about(arg_keys[1], (KEYS, C), 1.0, 6.0, ((0, 256),)),
        "patch_weight": scatter_about(arg_keys[2], (PP, E), PP ** -0.5, 0.75),
        "patch_bias": scatter_about(arg_keys[3], (E,), 0.7, 4.0, (), jnp.float32),
        "norm_gain": jnp.clip(1.0 + 0.18 * jax.random.normal(arg_keys[4], (E,), jnp.float32), 0.1, 1.9),
        "latent_queries": draw_latent_queries(jax.random.fold_in(arg_keys[9], 71), 0),
        "key_weight": scatter_about(arg_keys[6], (E, LD), E ** -0.5, 0.75),
        "value_weight": scatter_about(arg_keys[7], (E, LD), E ** -0.5, 0.75),
        "keep_mask": place_ends((jax.random.randint(arg_keys[8], (Q, PATCHES), 0, 2) < 1).astype(jnp.int32), jax.random.fold_in(arg_keys[8], 1), 0, 1),
    }


def encode_rows(query_rows, mask_rows, key_features, patch_weight, patch_bias, norm_gain, latent_queries, key_weight, value_weight):
    n_rows = query_rows.shape[0]
    cost_tile = lax.dot_general(query_rows, key_features, (((1,), (1,)), ((), ())), preferred_element_type=jnp.float32)
    cost_tile = (cost_tile / math.sqrt(C)).astype(jnp.bfloat16)
    cells = cost_tile.reshape(n_rows, PATCHES, PP).astype(jnp.float32)
    tokens = jnp.einsum('rtc,ce->rte', cells, patch_weight.astype(jnp.float32))
    tokens = tokens * mask_rows[:, :, None].astype(jnp.float32) + patch_bias
    centre = lax.optimization_barrier(jnp.mean(tokens, axis=2, keepdims=True))
    spread = lax.optimization_barrier(jnp.mean((tokens - centre) ** 2, axis=2, keepdims=True))
    normed = ((tokens - centre) / jnp.sqrt(spread + 1e-05) * norm_gain).astype(jnp.bfloat16)
    normed_f = normed.astype(jnp.float32)
    proj_keys = jnp.einsum('rte,ed->rtd', normed_f, key_weight.astype(jnp.float32))
    scores = jnp.einsum('rtd,ld->rlt', proj_keys, latent_queries, precision=lax.Precision.HIGHEST) / math.sqrt(LD)
    top_score = lax.optimization_barrier(jnp.max(scores, axis=2, keepdims=True))
    expo = jnp.exp(scores - top_score)
    denom = lax.optimization_barrier(jnp.sum(expo, axis=2))
    weighted = jnp.einsum('rlt,rte->rle', expo, normed_f, precision=lax.Precision.HIGHEST) / denom[:, :, None]
    pooled = weighted.astype(jnp.bfloat16)
    latent = jnp.einsum('rle,ed->rld', pooled.astype(jnp.float32), value_weight.astype(jnp.float32))
    return latent.astype(jnp.bfloat16)

def reference(query_features, key_features, patch_weight, patch_bias, norm_gain, latent_queries, key_weight, value_weight, keep_mask):
    blk_rows = math.gcd(Q, 64)
    n_blk = Q // blk_rows
    query_blocks = query_features.reshape(n_blk, blk_rows, C)
    mask_blocks = keep_mask.reshape(n_blk, blk_rows, PATCHES)

    def one_block(pair):
        return encode_rows(pair[0], pair[1], key_features, patch_weight, patch_bias, norm_gain, latent_queries, key_weight, value_weight)
    result = lax.map(one_block, (query_blocks, mask_blocks))
    return result.reshape(Q, LAT, LD)
```

```python
import math

import jax
import jax.numpy as jnp
from jax import lax
from jax.experimental import pallas as pl
from jax.experimental.pallas import tpu as pltpu
from jax.sharding import PartitionSpec as P

f32 = jnp.float32
bf16 = jnp.bfloat16
MESH = pl.DeviceIdType.MESH

NX, NZ, NY = 4, 8, 4
NQ, NT, CELLS, CH, E, LAT, LD = 640, 128, 64, 256, 64, 8, 128
NK = NT * CELLS
G = 32
NG = NQ // G
NP = G // 2
CHUNK = 128
NCH = NQ // CHUNK
GPC = CHUNK // G


def dot_nt(a, b):
    return lax.dot_general(a, b, (((1,), (1,)), ((), ())), preferred_element_type=f32)


def gather(me, y, k_ref, q_ref, kbuf, qbuf, ssem, rsem, qssem, qrsem, prepare):
    core = lax.rem(me, 2)
    z = lax.rem(lax.div(me, 2), NZ)
    x = lax.div(me, 2 * NZ)

    def pb(xx, zz, cc):
        return (lax.rem(xx + NX, NX) * NZ + lax.rem(zz + NZ, NZ)) * 2 + cc

    sibling = pb(x, z, 1 - core)
    ring = {"z+": pb(x, z + 1, core), "z-": pb(x, z - 1, core), "x+": pb(x + 1, z, core), "x-": pb(x - 1, z, core)}
    ring["s"] = sibling

    barrier = pltpu.get_barrier_semaphore()
    for other in ring.values():
        pl.semaphore_signal(barrier, inc=1, device_id=(other, y), device_id_type=MESH)
    for o in range(1, NY):
        pl.semaphore_signal(barrier, inc=1, device_id=(me, lax.rem(y + o, NY)), device_id_type=MESH)
    kbuf[me] = k_ref[...]
    qbuf[y] = q_ref[...]
    prepare()
    pl.semaphore_wait(barrier, len(ring) + NY - 1)

    def q_copy(o):
        return pltpu.make_async_remote_copy(
            src_ref=qbuf.at[y], dst_ref=qbuf.at[y], send_sem=qssem.at[o - 1], recv_sem=qrsem.at[o - 1],
            device_id=(me, lax.rem(y + o, NY)), device_id_type=MESH,
        )

    def copy(slot, to, sem):
        return pltpu.make_async_remote_copy(
            src_ref=kbuf.at[slot], dst_ref=kbuf.at[slot], send_sem=ssem.at[sem], recv_sem=rsem.at[slot],
            device_id=(to, y), device_id_type=MESH,
        )

    def run(route):
        count = [0]

        def send(slot, *ways):
            for way in ways:
                copy(slot, ring[way], count[0]).start()
                count[0] += 1

        def arrive(slot):
            copy(slot, sibling, 0).wait_recv()

        route(send, arrive)
        return count[0]

    def z_first(send, arrive):
        zs = [(z, None, 0), (z - 1, "z+", 1), (z + 1, "z-", 1), (z - 2, "z+", 2), (z + 2, "z-", 2), (z - 3, "z+", 3), (z + 3, "z-", 3), (z - 4, "z+", 4)]
        send(me, "z+", "z-", "x+", "x-", "s")
        for k in range(1, NZ + 2):
            if k < NZ:
                zz, way, dist = zs[k]
                slot = pb(x, zz, core)
                arrive(slot)
                if dist < (4 if way == "z+" else 3):
                    send(slot, way)
                send(slot, "x+", "x-", "s")
            if k <= NZ:
                i = k - 1
                slot = pb(x - 1, zs[i][0], core)
                arrive(slot)
                send(slot, *(("x+", "s") if i % 2 == 0 else ("s",)))
                slot = pb(x + 1, zs[i][0], core)
                arrive(slot)
                send(slot, *(("x-", "s") if i % 2 == 1 else ("s",)))
            if k >= 2:
                slot = pb(x + 2, zs[k - 2][0], core)
                arrive(slot)
                send(slot, "s")

    def x_first(send, arrive):
        send(me, "z+", "z-", "x+", "x-", "s")
        xs = [x, x - 1, x + 1, x + 2]
        for i in range(1, NX):
            slot = pb(xs[i], z, core)
            arrive(slot)
            if i == 1:
                send(slot, "x+")
            send(slot, "z+", "z-", "s")
        for dist in range(1, 5):
            for i in range(NX):
                last_plus, last_minus = (4, 3) if i < 2 else (3, 4)
                if dist <= last_plus:
                    slot = pb(xs[i], z - dist, core)
                    arrive(slot)
                    send(slot, *(("z+", "s") if dist < last_plus else ("s",)))
                if dist <= last_minus:
                    slot = pb(xs[i], z + dist, core)
                    arrive(slot)
                    send(slot, *(("z-", "s") if dist < last_minus else ("s",)))

    for o in range(1, NY):
        q_copy(o).start()

    @pl.when(core == 0)
    def _():
        assert run(z_first) == 63

    @pl.when(core == 1)
    def _():
        assert run(x_first) == 63

    @pl.loop(0, NX * NZ)
    def _(i):
        copy(2 * i + 1 - core, sibling, 0).wait_recv()

    for o in range(1, NY):
        q_copy(o).wait()

    @pl.loop(0, 63)
    def _(i):
        copy(me, sibling, i).wait_send()


def order_keys(kbuf, kf_ref, kp_ref):
    @pl.loop(0, NX * NZ * 2)
    def _(s):
        r = pl.multiple_of(s * 128, 128)
        for h in range(2):
            kf_ref[pl.ds(r + h * NK, 128), :] = kbuf[s, :, h * 128 : (h + 1) * 128].astype(f32)

    @pl.loop(0, CELLS)
    def _(c):
        for h in range(2):
            rows = pl.ds(pl.multiple_of(c * NT, NT), NT)
            kp_ref[rows, h * 128 : (h + 1) * 128] = kf_ref[pl.ds(c + h * NK, NT, stride=CELLS), :].astype(bf16)


def costs(qall, kp_ref, cost_ref):
    @pl.loop(0, NK // 512)
    def _(jj):
        for u in range(2):
            j = jj * 2 + u
            o = dot_nt(qall[...], kp_ref[pl.ds(pl.multiple_of(j * 256, 256), 256), :])
            for v in range(NQ // 4):
                for h in range(2):
                    cost_ref[pl.ds(v * 256 + (j * 2 + h) * 4, 4), :] = o[v * 4 : v * 4 + 4, h * 128 : (h + 1) * 128]


def pipeline(mask_ref, wd_ref, bias_ref, gain_ref, smap_ref, w_ref, lse_ref, cost_ref, toks, nrms, ps, ms, after):
    lane = lax.broadcasted_iota(jnp.int32, (8, 128), 1)
    sub = lax.broadcasted_iota(jnp.int32, (8, 128), 0)
    lane64 = lax.broadcasted_iota(jnp.int32, (64, 128), 1)

    def sums(g, slot):
        nrm_ref, p_ref, m_ref = nrms[slot], ps[slot], ms[slot]
        b2 = lax.rem(g + 1, 2) * 2
        zero = jnp.zeros((16, 128), bf16)
        rows = []
        for lp in range(LAT):
            st = jnp.bitwise_xor(b2, lp)
            pa = p_ref[pl.ds(st, 16, stride=8), :].astype(bf16)
            pb = p_ref[pl.ds(st + 128, 16, stride=8), :].astype(bf16)
            rows += [jnp.concatenate([pa, zero], axis=1), jnp.concatenate([zero, pb], axis=1)]
        pst = jnp.concatenate(rows, axis=0)
        acc = None
        for k in range(NP // 4):
            o = dot_nt(nrm_ref[k * 256 : (k + 1) * 256, :], pst)
            for i in range(4):
                ov = [o[i * 64 : (i + 1) * 64, v * 128 : (v + 1) * 128] for v in range(2)]
                own = lax.bitwise_and(lane64, 15) == k * 4 + i
                acc = ov if acc is None else [jnp.where(own, ov[v], acc[v]) for v in range(2)]
            if k < NP // 4 - 1:
                yield
        d = dot_nt(jnp.ones((16, 256), bf16), pst)[0:1, :]
        rd = 1.0 / d
        for v in range(2):
            vl = slice(v * 128, (v + 1) * 128)
            w_ref[pl.ds(pl.multiple_of(g * 64, 64), 64), vl] = acc[v] * rd[:, vl]
        lse_ref[pl.ds(pl.multiple_of(g * 8, 8), 8), :] = jnp.broadcast_to(m_ref[0:1, :] + jnp.log(d), (8, 256))
        yield

    def scores(g, slot):
        nrm_ref, p_ref, m_ref = nrms[slot], ps[slot], ms[slot]
        b2 = lax.rem(g, 2) * 2
        pos = lane - lax.bitwise_and(jnp.bitwise_xor(sub, b2), 3) * 32
        accm = jnp.zeros((8, 128), f32)
        for k in range(NP // 4):
            s3 = jnp.dot(smap_ref[...], nrm_ref[k * 256 : (k + 1) * 256, :], preferred_element_type=f32)
            for i in range(4):
                s = s3[24 * i : 24 * i + 8] + (s3[24 * i + 8 : 24 * i + 16] + s3[24 * i + 16 : 24 * i + 24])
                for h in range(2):
                    q = h * 16 + k * 4 + i
                    sq = s[:, h * 128 : (h + 1) * 128]
                    m = jnp.broadcast_to(jnp.max(sq, axis=1, keepdims=True), (8, 128))
                    p_ref[q * 8 : q * 8 + 8, :] = jnp.exp(sq - m)
                    accm = jnp.where(pos == q, m, accm)
            if k < NP // 4 - 1:
                yield
        m_ref[:, 0:128] = jnp.broadcast_to(jnp.sum(jnp.where(sub < 4, accm, 0.0), axis=0, keepdims=True), (8, 128))
        m_ref[:, 128:256] = jnp.broadcast_to(jnp.sum(jnp.where(sub < 4, 0.0, accm), axis=0, keepdims=True), (8, 128))
        yield

    def norms(slot):
        tok_ref, nrm_ref = toks[slot], nrms[slot]
        for i in range(NP):
            for h in range(2):
                hl = slice(h * 128, (h + 1) * 128)
                tok = tok_ref[i * 64 : (i + 1) * 64, hl] + bias_ref[:, hl]
                ss = jnp.sum(tok * tok, axis=0, keepdims=True)
                rstd = lax.rsqrt(ss * (1.0 / E) + 1e-5)
                nrm_ref[i * 64 : (i + 1) * 64, hl] = (tok * rstd * gain_ref[:, hl]).astype(bf16)
                yield

    def tokens(g, slot):
        q0 = jnp.minimum(g, NG - 1) * G
        for k in range(NP // 2):
            rows = []
            for i in range(2):
                xs = []
                for h in range(2):
                    q = h * 16 + k * 2 + i
                    base = pl.multiple_of((q0 + q // 4 * 4) * CELLS, 256) + q % 4
                    xq = cost_ref[pl.ds(base, CELLS, stride=4), :].astype(bf16)
                    mk = jnp.broadcast_to(mask_ref[pl.ds(q0 + q, 1), :].astype(f32), (CELLS, NT)).astype(bf16)
                    xs.append(xq * mk)
                xx = jnp.concatenate(xs, axis=1)
                rows += [xx, xx]
            toks[slot][k * 128 : (k + 1) * 128, :] = jnp.dot(
                wd_ref[...], jnp.concatenate(rows, axis=0), preferred_element_type=f32
            )
            yield

    @pl.loop(0, (NG + 3 + 2) // 3)
    def _(it):
        for u in range(3):
            g = it * 3 + u

            @pl.when(g < NG + 3)
            def _():
                steps = {
                    "w": sums(g, u), "s": scores(g, (u + 1) % 3), "n": norms((u + 2) % 3), "t": tokens(g, u),
                }
                for step in "snn" * 4 + "wnnnn" * 4 + "tn" * 8:
                    next(steps[step])
                after(g)


def split(a, n):
    parts = []
    for _ in range(n):
        parts.append(a.astype(bf16).astype(f32))
        a = a - parts[-1]
    return parts


def parameters(weight_ref, pbias_ref, pgain_ref, latq_ref, key_ref, wd_ref, bias_ref, gain_ref, smap_ref):
    weight = weight_ref[...].astype(f32).T
    centred = (weight - jnp.mean(weight, axis=0, keepdims=True)) / math.sqrt(CH)
    parts = jnp.concatenate(split(centred, 2), axis=1)
    zero = jnp.zeros((E, 128), f32)
    wd_ref[...] = jnp.concatenate(
        [jnp.concatenate([parts, zero], axis=1), jnp.concatenate([zero, parts], axis=1)], axis=0
    ).astype(bf16)
    bias = pbias_ref[...]
    bias = bias - jnp.mean(bias, axis=1, keepdims=True)
    for source, ref in ((bias, bias_ref), (pgain_ref[...], gain_ref)):
        column = jnp.broadcast_to(source, (128, E)).T
        ref[:, 0:128] = column
        ref[:, 128:256] = column
    score_map = lax.dot_general(
        latq_ref[...], key_ref[...].astype(f32), (((1,), (1,)), ((), ())),
        precision=lax.Precision.HIGHEST, preferred_element_type=f32,
    ) / math.sqrt(LD)
    parts = jnp.concatenate(split(score_map, 3), axis=0)
    zero = jnp.zeros_like(parts)
    smap_ref[...] = jnp.concatenate(
        [jnp.concatenate([parts if i == j else zero for j in range(4)], axis=1) for i in range(4)], axis=0
    ).astype(bf16)


def kernel(
    q_ref, k_ref, mask_ref, weight_ref, pbias_ref, pgain_ref, latq_ref, key_ref, value_ref, out_ref,
    kbuf, qbuf, kf_ref, kp_ref, qall, cost_ref, toks, nrms, ps, ms, w_ref, lse_ref, wd_ref, bias_ref, gain_ref, smap_ref,
    sbuf, sst, rbuf, rst, ssem, rsem, qssem, qrsem, dssem, drsem, tssem, trsem,
):
    me = lax.axis_index("pb")
    y = lax.axis_index("ka")
    def prepare():
        parameters(weight_ref, pbias_ref, pgain_ref, latq_ref, key_ref, wd_ref, bias_ref, gain_ref, smap_ref)
        for refs in (ps, ms, nrms, toks):
            for ref in refs:
                ref[...] = jnp.ones_like(ref)

    gather(me, y, k_ref, q_ref, kbuf, qbuf, ssem, rsem, qssem, qrsem, prepare)
    qall[...] = jnp.concatenate([qbuf[i] for i in range(NY)], axis=0).astype(f32).T.astype(bf16)
    order_keys(kbuf, kf_ref, kp_ref)
    costs(qall, kp_ref, cost_ref)
    lane64 = lax.broadcasted_iota(jnp.int32, (64, 128), 1)
    lane8 = lax.broadcasted_iota(jnp.int32, (8, 128), 1)

    def copies(k, o):
        to = lax.rem(y + o, NY)
        rows = pl.ds(pl.multiple_of(k * 128, 128), 128)
        st = pl.ds(pl.multiple_of(k * 16, 16), 16)
        return (
            pltpu.make_async_remote_copy(
                src_ref=sbuf.at[to, rows], dst_ref=rbuf.at[o - 1, rows], send_sem=dssem.at[o - 1, k],
                recv_sem=drsem.at[o - 1, k], device_id=(me, to), device_id_type=MESH,
            ),
            pltpu.make_async_remote_copy(
                src_ref=sst.at[to, st], dst_ref=rst.at[o - 1, st], send_sem=tssem.at[o - 1, k],
                recv_sem=trsem.at[o - 1, k], device_id=(me, to), device_id_type=MESH,
            ),
        )

    def send_chunk(k):
        for blk in range(2):
            ga = k * GPC + blk * 2 + 3
            for v in range(2):
                vl = slice(v * 128, (v + 1) * 128)
                wa = w_ref[pl.ds(pl.multiple_of(ga * 64, 64), 64), vl]
                wb = w_ref[pl.ds(pl.multiple_of(ga * 64 + 64, 64), 64), vl]
                la = lse_ref[pl.ds(pl.multiple_of(ga * 8, 8), 8), vl]
                lb = lse_ref[pl.ds(pl.multiple_of(ga * 8 + 8, 8), 8), vl]
                rows = pl.ds(pl.multiple_of(k * 128 + blk * 64, 64), 64)
                st = pl.ds(pl.multiple_of(k * 16 + blk * 8, 8), 8)
                sbuf[2 * v, rows, :] = jnp.where(lane64 < 64, wa, wb).astype(bf16)
                sbuf[2 * v + 1, rows, :] = jnp.where(lane64 < 64, wb, wa).astype(bf16)
                sst[2 * v, st, :] = jnp.where(lane8 < 64, la, lb)
                sst[2 * v + 1, st, :] = jnp.where(lane8 < 64, lb, la)
        for o in range(1, NY):
            for c in copies(k, o):
                c.start()

    def combine_chunk(k):
        for o in range(1, NY):
            for c in copies(k, o):
                c.wait_recv()
        odd = lax.rem(y, 2)
        for blk in range(2):
            rows = pl.ds(pl.multiple_of(k * 128 + blk * 64, 64), 64)
            st = pl.ds(pl.multiple_of(k * 16 + blk * 8, 8), 8)
            lses = [sst[y, st, :]] + [rst[o, st, :] for o in range(NY - 1)]
            vals = [sbuf[y, rows, :]] + [rbuf[o, rows, :] for o in range(NY - 1)]
            top = jnp.maximum(jnp.maximum(lses[0], lses[1]), jnp.maximum(lses[2], lses[3]))
            facs = [jnp.exp(a - top) for a in lses]
            inv = 1.0 / (facs[0] + facs[1] + facs[2] + facs[3])
            pooled = sum(v.astype(f32) * (a * inv)[0:1, :] for v, a in zip(vals, facs))
            res = lax.dot_general(
                pooled.astype(bf16), value_ref[...], (((0,), (0,)), ((), ())), preferred_element_type=f32
            ).astype(bf16)
            for half in range(2):
                off = odd * 32 if half == 0 else (1 - odd) * 32
                orow = pl.ds(pl.multiple_of(k * 128 + blk * 64 + off, 32), 32)
                for l in range(2):
                    r = (half * 2 + l) * 32
                    out_ref[orow, l * 128 : (l + 1) * 128] = res[r : r + 32, :]

    def after(g):
        @pl.when(jnp.logical_and(lax.rem(g, GPC) == 2, g > 3))
        def _():
            k = lax.div(g - 3, GPC)
            send_chunk(k)

            @pl.when(k > 0)
            def _():
                combine_chunk(k - 1)

    pipeline(mask_ref, wd_ref, bias_ref, gain_ref, smap_ref, w_ref, lse_ref, cost_ref, toks, nrms, ps, ms, after)
    combine_chunk(NCH - 1)

    @pl.loop(0, NCH)
    def _(k):
        for o in range(1, NY):
            for c in copies(k, o):
                c.wait_send()


def body(
    query_features, key_features, patch_weight, patch_bias, norm_gain, latent_queries, key_weight, value_weight, keep_mask
):
    vmem = pl.BlockSpec(memory_space=pltpu.VMEM)
    dma = pltpu.SemaphoreType.DMA
    out = pl.pallas_call(
        kernel,
        out_shape=jax.ShapeDtypeStruct((NQ, 2 * LD), bf16),
        in_specs=[vmem] * 9,
        out_specs=vmem,
        scratch_shapes=[
            pltpu.VMEM((2 * NX * NZ, 128, CH), bf16),
            pltpu.VMEM((NY, CH // NY, NQ), bf16),
            pltpu.VMEM((2 * NK, 128), f32),
            pltpu.VMEM((NK, CH), bf16),
            pltpu.VMEM((NQ, CH), bf16),
            pltpu.VMEM((CELLS * NQ, NT), f32),
            [pltpu.VMEM((NP * E, 256), f32)] * 3,
            [pltpu.VMEM((NP * E, 256), bf16)] * 3,
            [pltpu.VMEM((G * LAT, NT), f32)] * 3,
            [pltpu.VMEM((8, 256), f32)] * 3,
            pltpu.VMEM(((NG + 3) * E, 256), f32),
            pltpu.VMEM(((NG + 3) * 8, 256), f32),
            pltpu.VMEM((2 * E, 256), bf16),
            pltpu.VMEM((E, 256), f32),
            pltpu.VMEM((E, 256), f32),
            pltpu.VMEM((96, 256), bf16),
            pltpu.VMEM((NY, NQ, 128), bf16),
            pltpu.VMEM((NY, NCH * 16, 128), f32),
            pltpu.VMEM((NY - 1, NQ, 128), bf16),
            pltpu.VMEM((NY - 1, NCH * 16, 128), f32),
            dma((64,)),
            dma((64,)),
            dma((NY - 1,)),
            dma((NY - 1,)),
            dma((NY - 1, NCH)),
            dma((NY - 1, NCH)),
            dma((NY - 1, NCH)),
            dma((NY - 1, NCH)),
        ],
        compiler_params=pltpu.CompilerParams(
            collective_id=0, has_side_effects=True, vmem_limit_bytes=60 * 1024 * 1024
        ),
    )(
        query_features.T, key_features, keep_mask, patch_weight, patch_bias.reshape(1, E), norm_gain.reshape(1, E),
        latent_queries, key_weight, value_weight,
    )
    return out.reshape(NQ, 2, LD)


def solution(mesh):
    placed = (P("pb", "ka"), P(("ka", "pb"), None), P(), P(), P(), P(), P(), P(), P("pb", "ka"))
    return jax.shard_map(
        body, mesh=mesh, in_specs=placed, out_specs=P("pb", "ka", None), check_vma=False
    )
```

```python
import math

import jax
import jax.numpy as jnp
from jax import lax
from jax.experimental import pallas as pl
from jax.experimental.pallas import tpu as pltpu
from jax.sharding import PartitionSpec as P

f32 = jnp.float32
bf16 = jnp.bfloat16
MESH = pl.DeviceIdType.MESH

NX, NZ, NY = 4, 8, 4
NQ, NT, CELLS, CH, E, LAT, LD = 640, 128, 64, 256, 64, 8, 128
NK = NT * CELLS
G = 32
NG = NQ // G
NP = G // 2
CHUNK = 128
NCH = NQ // CHUNK
GPC = CHUNK // G


def dot_nt(a, b):
    return lax.dot_general(a, b, (((1,), (1,)), ((), ())), preferred_element_type=f32)


def gather(me, y, k_ref, q_ref, kbuf, qbuf, ssem, rsem, qssem, qrsem, prepare, queries):
    core = lax.rem(me, 2)
    z = lax.rem(lax.div(me, 2), NZ)
    x = lax.div(me, 2 * NZ)

    def pb(xx, zz, cc):
        return (lax.rem(xx + NX, NX) * NZ + lax.rem(zz + NZ, NZ)) * 2 + cc

    sibling = pb(x, z, 1 - core)
    ring = {f"z{d}": pb(x, z + d, core) for d in range(1, NZ)}
    ring.update({"x+": pb(x + 1, z, core), "x-": pb(x - 1, z, core), "x2": pb(x + 2, z, core), "s": sibling})

    barrier = pltpu.get_barrier_semaphore()
    for other in ring.values():
        pl.semaphore_signal(barrier, inc=1, device_id=(other, y), device_id_type=MESH)
    for o in range(1, NY):
        pl.semaphore_signal(barrier, inc=1, device_id=(me, lax.rem(y + o, NY)), device_id_type=MESH)
    kbuf[me] = k_ref[...]
    qbuf[y] = q_ref[...]
    prepare()
    pl.semaphore_wait(barrier, len(ring) + NY - 1)

    def q_copy(o):
        return pltpu.make_async_remote_copy(
            src_ref=qbuf.at[y], dst_ref=qbuf.at[y], send_sem=qssem.at[o - 1], recv_sem=qrsem.at[o - 1],
            device_id=(me, lax.rem(y + o, NY)), device_id_type=MESH,
        )

    def copy(slot, to, sem):
        return pltpu.make_async_remote_copy(
            src_ref=kbuf.at[slot], dst_ref=kbuf.at[slot], send_sem=ssem.at[sem], recv_sem=rsem.at[slot],
            device_id=(to, y), device_id_type=MESH,
        )

    def run(route):
        count = [0]

        def send(slot, *ways):
            for way in ways:
                copy(slot, ring[way], count[0]).start()
                count[0] += 1

        def arrive(slot):
            copy(slot, sibling, 0).wait_recv()

        route(send, arrive)
        return count[0]

    def z_first(send, arrive):
        zs = [z, z - 1, z + 1, z - 2, z + 2, z - 3, z + 3, z - 4]
        send(me, *(f"z{d}" for d in (1, 7, 2, 6, 3, 5, 4)), "x+", "x-", "s")
        for zz in zs[1:]:
            slot = pb(x, zz, core)
            arrive(slot)
            send(slot, "x+", "x-", "s")
        for i, zz in enumerate(zs):
            slot = pb(x - 1, zz, core)
            arrive(slot)
            send(slot, *(("x+", "s") if i % 2 == 0 else ("s",)))
            slot = pb(x + 1, zz, core)
            arrive(slot)
            send(slot, *(("x-", "s") if i % 2 == 1 else ("s",)))
        for zz in zs:
            slot = pb(x + 2, zz, core)
            arrive(slot)
            send(slot, "s")

    def x_first(send, arrive):
        send(me, "z1", "z7", "x+", "x-", "x2", "s")
        xs = [x, x - 1, x + 1, x + 2]
        for i in range(1, NX):
            slot = pb(xs[i], z, core)
            arrive(slot)
            send(slot, "z1", "z7", "s")
        for dist in range(1, 5):
            for i in range(NX):
                last_plus, last_minus = (4, 3) if i < 2 else (3, 4)
                if dist <= last_plus:
                    slot = pb(xs[i], z - dist, core)
                    arrive(slot)
                    send(slot, *(("z1", "s") if dist < last_plus else ("s",)))
                if dist <= last_minus:
                    slot = pb(xs[i], z + dist, core)
                    arrive(slot)
                    send(slot, *(("z7", "s") if dist < last_minus else ("s",)))

    for o in range(1, NY):
        q_copy(o).start()

    @pl.when(core == 0)
    def _():
        assert run(z_first) == 63

    @pl.when(core == 1)
    def _():
        assert run(x_first) == 63

    for o in range(1, NY):
        q_copy(o).wait()
    queries()

    @pl.loop(0, NX * NZ)
    def _(i):
        copy(2 * i + 1 - core, sibling, 0).wait_recv()

    @pl.loop(0, 63)
    def _(i):
        copy(me, sibling, i).wait_send()


def order_keys(kbuf, kf_ref, kp_ref):
    @pl.loop(0, NX * NZ * 2)
    def _(s):
        for i in range(2):
            base = lax.div(s, 4) * 512 + (lax.rem(s, 4) * 2 + i) * 8
            for c in range(CELLS // 8):
                for h in range(2):
                    to = pl.multiple_of(base + c * 64, 8) + h * NK
                    kf_ref[pl.ds(to, 8), :] = kbuf[s, i * CELLS + c * 8 : i * CELLS + c * 8 + 8, h * 128 : (h + 1) * 128].astype(f32)

    @pl.loop(0, CELLS // 4)
    def _(i):
        for u in range(4):
            base = pl.multiple_of(lax.div(i, 2) * 64, 64) + lax.rem(i, 2) * 4 + u
            for h in range(2):
                for t in range(0, NT // 8, 2):
                    pair = [kf_ref[pl.ds(base + (t + j) * 512 + h * NK, 8, stride=8), :] for j in range(2)]
                    rows = pl.ds(pl.multiple_of((i * 4 + (0, 2, 1, 3)[u]) * NT + t * 8, 16), 16)
                    kp_ref[rows, h * 128 : (h + 1) * 128] = jnp.concatenate(pair, axis=0).astype(bf16)


def costs(qall, kp_ref, cost_ref):
    low = lax.broadcasted_iota(jnp.int32, (8, 128), 0) < 4

    @pl.loop(0, CELLS // 4)
    def _(j):
        r = pl.multiple_of(j * 512, 512)
        even = dot_nt(qall[0], kp_ref[pl.ds(r, 256), :])
        odd = dot_nt(qall[1], kp_ref[pl.ds(r + 256, 256), :])
        for v in range(NQ // 8):
            for h in range(2):
                ev = even[v * 8 : v * 8 + 8, h * 128 : (h + 1) * 128]
                od = odd[v * 8 : v * 8 + 8, h * 128 : (h + 1) * 128]
                to = pl.multiple_of(v * 512 + j * 16 + h * 8, 8)
                cost_ref[pl.ds(to, 8), :] = jnp.where(low, ev, od)
                cost_ref[pl.ds(to + 256, 8), :] = jnp.where(low, od, ev)


def pipeline(mask_ref, wd_ref, bias_ref, gain_ref, smap_ref, w_ref, lse_ref, cost_ref, toks, nrms, ps, ms, after):
    lane = lax.broadcasted_iota(jnp.int32, (8, 128), 1)
    sub = lax.broadcasted_iota(jnp.int32, (8, 128), 0)
    lane64 = lax.broadcasted_iota(jnp.int32, (64, 128), 1)

    def sums(g, slot):
        nrm_ref, p_ref, m_ref = nrms[slot], ps[slot], ms[slot]
        b2 = lax.rem(g + 1, 2) * 2
        zero = jnp.zeros((16, 128), bf16)
        rows = []
        for lp in range(LAT):
            st = jnp.bitwise_xor(b2, lp)
            pa = p_ref[pl.ds(st, 16, stride=8), :].astype(bf16)
            pb = p_ref[pl.ds(st + 128, 16, stride=8), :].astype(bf16)
            rows += [jnp.concatenate([pa, zero], axis=1), jnp.concatenate([zero, pb], axis=1)]
        pst = jnp.concatenate(rows, axis=0)
        o = dot_nt(jnp.concatenate([nrm_ref[...], jnp.ones((16, 256), bf16)], axis=0), pst)
        acc = None
        for p in range(NP):
            ov = [o[p * 64 : (p + 1) * 64, v * 128 : (v + 1) * 128] for v in range(2)]
            own = lax.bitwise_and(lane64, 15) == p
            acc = ov if acc is None else [jnp.where(own, ov[v], acc[v]) for v in range(2)]
        d = o[NP * 64 : NP * 64 + 1, :]
        rd = 1.0 / d
        for v in range(2):
            vl = slice(v * 128, (v + 1) * 128)
            w_ref[pl.ds(pl.multiple_of(g * 64, 64), 64), vl] = acc[v] * rd[:, vl]
        lse_ref[pl.ds(pl.multiple_of(g * 8, 8), 8), :] = jnp.broadcast_to(m_ref[0:1, :] + jnp.log(d), (8, 256))
        yield

    def scores(g, slot):
        nrm_ref, p_ref, m_ref = nrms[slot], ps[slot], ms[slot]
        b2 = lax.rem(g, 2) * 2
        pos = lane - lax.bitwise_and(jnp.bitwise_xor(sub, b2), 3) * 32
        accm = jnp.zeros((8, 128), f32)
        for k in range(NP // 4):
            s3 = jnp.dot(smap_ref[...], nrm_ref[k * 256 : (k + 1) * 256, :], preferred_element_type=f32)
            for i in range(4):
                s = s3[24 * i : 24 * i + 8] + (s3[24 * i + 8 : 24 * i + 16] + s3[24 * i + 16 : 24 * i + 24])
                for h in range(2):
                    q = h * 16 + k * 4 + i
                    sq = s[:, h * 128 : (h + 1) * 128]
                    m = jnp.broadcast_to(jnp.max(sq, axis=1, keepdims=True), (8, 128))
                    p_ref[q * 8 : q * 8 + 8, :] = jnp.exp(sq - m)
                    accm = jnp.where(pos == q, m, accm)
            if k < NP // 4 - 1:
                yield
        m_ref[:, 0:128] = jnp.broadcast_to(jnp.sum(jnp.where(sub < 4, accm, 0.0), axis=0, keepdims=True), (8, 128))
        m_ref[:, 128:256] = jnp.broadcast_to(jnp.sum(jnp.where(sub < 4, 0.0, accm), axis=0, keepdims=True), (8, 128))
        yield

    def norms(slot):
        tok_ref, nrm_ref = toks[slot], nrms[slot]
        for i in range(NP):
            for h in range(2):
                hl = slice(h * 128, (h + 1) * 128)
                tok = tok_ref[i * 64 : (i + 1) * 64, hl] + bias_ref[:, hl]
                ss = jnp.sum(tok * tok, axis=0, keepdims=True)
                rstd = lax.rsqrt(ss * (1.0 / E) + 1e-5)
                nrm_ref[i * 64 : (i + 1) * 64, hl] = (tok * rstd * gain_ref[:, hl]).astype(bf16)
                yield

    def tokens(g, slot):
        q0 = jnp.minimum(g, NG - 1) * G
        for k in range(NP // 2):
            rows = []
            for i in range(2):
                xs = []
                for h in range(2):
                    q = h * 16 + k * 2 + i
                    base = pl.multiple_of((q0 + q // 4 * 4) * CELLS, 256) + q % 4
                    xq = cost_ref[pl.ds(base, CELLS, stride=4), :].astype(bf16)
                    mk = jnp.broadcast_to(mask_ref[pl.ds(q0 + q, 1), :].astype(f32), (CELLS, NT)).astype(bf16)
                    xs.append(xq * mk)
                xx = jnp.concatenate(xs, axis=1)
                rows += [xx, xx]
            toks[slot][k * 128 : (k + 1) * 128, :] = jnp.dot(
                wd_ref[k % 4 // 2], jnp.concatenate(rows, axis=0), preferred_element_type=f32
            )
            yield

    @pl.loop(0, (NG + 3 + 2) // 3)
    def _(it):
        for u in range(3):
            g = it * 3 + u

            @pl.when(g < NG + 3)
            def _():
                steps = {
                    "w": sums(g, u), "s": scores(g, (u + 1) % 3), "n": norms((u + 2) % 3), "t": tokens(g, u),
                }
                for step in "w" + "n" * 16 + "snn" * 4 + "tn" * 8:
                    next(steps[step])
                after(g)


def split(a, n):
    parts = []
    for _ in range(n):
        parts.append(a.astype(bf16).astype(f32))
        a = a - parts[-1]
    return parts


def parameters(weight_ref, pbias_ref, pgain_ref, latq_ref, key_ref, wd_ref, bias_ref, gain_ref, smap_ref):
    weight = weight_ref[...].astype(f32)
    even = lax.rem(lax.broadcasted_iota(jnp.int32, (CELLS, E), 0), 2) == 0
    swapped = jnp.where(even, pltpu.roll(weight, CELLS - 1, 0), pltpu.roll(weight, 1, 0))
    zero = jnp.zeros((E, 128), f32)
    for i, form in enumerate((weight, swapped)):
        form = form.T
        centred = (form - jnp.mean(form, axis=0, keepdims=True)) / math.sqrt(CH)
        parts = jnp.concatenate(split(centred, 2), axis=1)
        wd_ref[i] = jnp.concatenate(
            [jnp.concatenate([parts, zero], axis=1), jnp.concatenate([zero, parts], axis=1)], axis=0
        ).astype(bf16)
    bias = pbias_ref[...]
    bias = bias - jnp.mean(bias, axis=1, keepdims=True)
    for source, ref in ((bias, bias_ref), (pgain_ref[...], gain_ref)):
        column = jnp.broadcast_to(source, (128, E)).T
        ref[:, 0:128] = column
        ref[:, 128:256] = column
    score_map = lax.dot_general(
        latq_ref[...], key_ref[...].astype(f32), (((1,), (1,)), ((), ())),
        precision=lax.Precision.HIGHEST, preferred_element_type=f32,
    ) / math.sqrt(LD)
    parts = jnp.concatenate(split(score_map, 3), axis=0)
    zero = jnp.zeros_like(parts)
    smap_ref[...] = jnp.concatenate(
        [jnp.concatenate([parts if i == j else zero for j in range(4)], axis=1) for i in range(4)], axis=0
    ).astype(bf16)


def kernel(
    q_ref, k_ref, mask_ref, weight_ref, pbias_ref, pgain_ref, latq_ref, key_ref, value_ref, out_ref,
    kbuf, qbuf, kf_ref, kp_ref, qall, cost_ref, toks, nrms, ps, ms, w_ref, lse_ref, wd_ref, bias_ref, gain_ref, smap_ref,
    sbuf, sst, rbuf, rst, ssem, rsem, qssem, qrsem, dssem, drsem, tssem, trsem,
):
    me = lax.axis_index("pb")
    y = lax.axis_index("ka")
    def prepare():
        parameters(weight_ref, pbias_ref, pgain_ref, latq_ref, key_ref, wd_ref, bias_ref, gain_ref, smap_ref)
        for refs in (ps, ms, nrms, toks):
            for ref in refs:
                ref[...] = jnp.ones_like(ref)

    def queries():
        rows = jnp.concatenate([qbuf[i] for i in range(NY)], axis=0).astype(f32).T
        qall[0] = rows.astype(bf16)
        qall[1] = pltpu.roll(rows.reshape(NQ // 8, 8, CH), 4, 1).reshape(NQ, CH).astype(bf16)

    gather(me, y, k_ref, q_ref, kbuf, qbuf, ssem, rsem, qssem, qrsem, prepare, queries)
    order_keys(kbuf, kf_ref, kp_ref)
    costs(qall, kp_ref, cost_ref)
    lane64 = lax.broadcasted_iota(jnp.int32, (64, 128), 1)
    lane8 = lax.broadcasted_iota(jnp.int32, (8, 128), 1)

    def copies(k, o):
        to = lax.rem(y + o, NY)
        rows = pl.ds(pl.multiple_of(k * 128, 128), 128)
        st = pl.ds(pl.multiple_of(k * 16, 16), 16)
        return (
            pltpu.make_async_remote_copy(
                src_ref=sbuf.at[to, rows], dst_ref=rbuf.at[o - 1, rows], send_sem=dssem.at[o - 1, k],
                recv_sem=drsem.at[o - 1, k], device_id=(me, to), device_id_type=MESH,
            ),
            pltpu.make_async_remote_copy(
                src_ref=sst.at[to, st], dst_ref=rst.at[o - 1, st], send_sem=tssem.at[o - 1, k],
                recv_sem=trsem.at[o - 1, k], device_id=(me, to), device_id_type=MESH,
            ),
        )

    def send_chunk(k):
        for blk in range(2):
            ga = k * GPC + blk * 2 + 3
            for v in range(2):
                vl = slice(v * 128, (v + 1) * 128)
                wa = w_ref[pl.ds(pl.multiple_of(ga * 64, 64), 64), vl]
                wb = w_ref[pl.ds(pl.multiple_of(ga * 64 + 64, 64), 64), vl]
                la = lse_ref[pl.ds(pl.multiple_of(ga * 8, 8), 8), vl]
                lb = lse_ref[pl.ds(pl.multiple_of(ga * 8 + 8, 8), 8), vl]
                rows = pl.ds(pl.multiple_of(k * 128 + blk * 64, 64), 64)
                st = pl.ds(pl.multiple_of(k * 16 + blk * 8, 8), 8)
                sbuf[2 * v, rows, :] = jnp.where(lane64 < 64, wa, wb).astype(bf16)
                sbuf[2 * v + 1, rows, :] = jnp.where(lane64 < 64, wb, wa).astype(bf16)
                sst[2 * v, st, :] = jnp.where(lane8 < 64, la, lb)
                sst[2 * v + 1, st, :] = jnp.where(lane8 < 64, lb, la)
        for o in range(1, NY):
            for c in copies(k, o):
                c.start()

    def combine_chunk(k):
        for o in range(1, NY):
            for c in copies(k, o):
                c.wait_recv()
        odd = lax.rem(y, 2)
        for blk in range(2):
            rows = pl.ds(pl.multiple_of(k * 128 + blk * 64, 64), 64)
            st = pl.ds(pl.multiple_of(k * 16 + blk * 8, 8), 8)
            lses = [sst[y, st, :]] + [rst[o, st, :] for o in range(NY - 1)]
            vals = [sbuf[y, rows, :]] + [rbuf[o, rows, :] for o in range(NY - 1)]
            top = jnp.maximum(jnp.maximum(lses[0], lses[1]), jnp.maximum(lses[2], lses[3]))
            facs = [jnp.exp(a - top) for a in lses]
            inv = 1.0 / (facs[0] + facs[1] + facs[2] + facs[3])
            pooled = sum(v.astype(f32) * (a * inv)[0:1, :] for v, a in zip(vals, facs))
            res = lax.dot_general(
                pooled.astype(bf16), value_ref[...], (((0,), (0,)), ((), ())), preferred_element_type=f32
            ).astype(bf16)
            for half in range(2):
                off = odd * 32 if half == 0 else (1 - odd) * 32
                orow = pl.ds(pl.multiple_of(k * 128 + blk * 64 + off, 32), 32)
                for l in range(2):
                    r = (half * 2 + l) * 32
                    out_ref[orow, l * 128 : (l + 1) * 128] = res[r : r + 32, :]

    def after(g):
        @pl.when(jnp.logical_and(lax.rem(g, GPC) == 2, g > 3))
        def _():
            k = lax.div(g - 3, GPC)
            send_chunk(k)

    pipeline(mask_ref, wd_ref, bias_ref, gain_ref, smap_ref, w_ref, lse_ref, cost_ref, toks, nrms, ps, ms, after)

    @pl.loop(0, NCH)
    def _(k):
        combine_chunk(k)

    @pl.loop(0, NCH)
    def _(k):
        for o in range(1, NY):
            for c in copies(k, o):
                c.wait_send()


def body(
    query_features, key_features, patch_weight, patch_bias, norm_gain, latent_queries, key_weight, value_weight, keep_mask
):
    vmem = pl.BlockSpec(memory_space=pltpu.VMEM)
    dma = pltpu.SemaphoreType.DMA
    out = pl.pallas_call(
        kernel,
        out_shape=jax.ShapeDtypeStruct((NQ, 2 * LD), bf16),
        in_specs=[vmem] * 9,
        out_specs=vmem,
        scratch_shapes=[
            pltpu.VMEM((2 * NX * NZ, 128, CH), bf16),
            pltpu.VMEM((NY, CH // NY, NQ), bf16),
            pltpu.VMEM((2 * NK, 128), f32),
            pltpu.VMEM((NK, CH), bf16),
            pltpu.VMEM((2, NQ, CH), bf16),
            pltpu.VMEM((CELLS * NQ, NT), f32),
            [pltpu.VMEM((NP * E, 256), f32)] * 3,
            [pltpu.VMEM((NP * E, 256), bf16)] * 3,
            [pltpu.VMEM((G * LAT, NT), f32)] * 3,
            [pltpu.VMEM((8, 256), f32)] * 3,
            pltpu.VMEM(((NG + 3) * E, 256), f32),
            pltpu.VMEM(((NG + 3) * 8, 256), f32),
            pltpu.VMEM((2, 2 * E, 256), bf16),
            pltpu.VMEM((E, 256), f32),
            pltpu.VMEM((E, 256), f32),
            pltpu.VMEM((96, 256), bf16),
            pltpu.VMEM((NY, NQ, 128), bf16),
            pltpu.VMEM((NY, NCH * 16, 128), f32),
            pltpu.VMEM((NY - 1, NQ, 128), bf16),
            pltpu.VMEM((NY - 1, NCH * 16, 128), f32),
            dma((64,)),
            dma((64,)),
            dma((NY - 1,)),
            dma((NY - 1,)),
            dma((NY - 1, NCH)),
            dma((NY - 1, NCH)),
            dma((NY - 1, NCH)),
            dma((NY - 1, NCH)),
        ],
        compiler_params=pltpu.CompilerParams(
            collective_id=0, has_side_effects=True, vmem_limit_bytes=60 * 1024 * 1024
        ),
    )(
        query_features.T, key_features, keep_mask, patch_weight, patch_bias.reshape(1, E), norm_gain.reshape(1, E),
        latent_queries, key_weight, value_weight,
    )
    return out.reshape(NQ, 2, LD)


def solution(mesh):
    placed = (P("pb", "ka"), P(("ka", "pb"), None), P(), P(), P(), P(), P(), P(), P("pb", "ka"))
    return jax.shard_map(
        body, mesh=mesh, in_specs=placed, out_specs=P("pb", "ka", None), check_vma=False
    )
```

```python
import math

import jax
import jax.numpy as jnp
from jax import lax
from jax.experimental import pallas as pl
from jax.experimental.pallas import tpu as pltpu
from jax.sharding import PartitionSpec as P

f32 = jnp.float32
bf16 = jnp.bfloat16
MESH = pl.DeviceIdType.MESH

NX, NZ, NY = 4, 8, 4
NQ, NT, CELLS, CH, E, LAT, LD = 640, 128, 64, 256, 64, 8, 128
NK = NT * CELLS
G = 32
NG = NQ // G
NP = G // 2
CHUNK = 128
NCH = NQ // CHUNK
GPC = CHUNK // G


def dot_nt(a, b):
    return lax.dot_general(a, b, (((1,), (1,)), ((), ())), preferred_element_type=f32)


def gather(me, y, k_ref, q_ref, kbuf, qbuf, ssem, rsem, qssem, qrsem, prepare, queries, landed):
    core = lax.rem(me, 2)
    z = lax.rem(lax.div(me, 2), NZ)
    x = lax.div(me, 2 * NZ)

    def pb(xx, zz, cc):
        return (lax.rem(xx + NX, NX) * NZ + lax.rem(zz + NZ, NZ)) * 2 + cc

    sibling = pb(x, z, 1 - core)
    ring = {f"z{d}": pb(x, z + d, core) for d in range(1, NZ)}
    ring.update({"x+": pb(x + 1, z, core), "x-": pb(x - 1, z, core), "x2": pb(x + 2, z, core), "s": sibling})

    barrier = pltpu.get_barrier_semaphore()
    for other in ring.values():
        pl.semaphore_signal(barrier, inc=1, device_id=(other, y), device_id_type=MESH)
    for o in range(1, NY):
        pl.semaphore_signal(barrier, inc=1, device_id=(me, lax.rem(y + o, NY)), device_id_type=MESH)
    kbuf[me] = k_ref[...]
    qbuf[y] = q_ref[...]
    prepare()
    pl.semaphore_wait(barrier, len(ring) + NY - 1)

    def q_copy(o):
        return pltpu.make_async_remote_copy(
            src_ref=qbuf.at[y], dst_ref=qbuf.at[y], send_sem=qssem.at[o - 1], recv_sem=qrsem.at[o - 1],
            device_id=(me, lax.rem(y + o, NY)), device_id_type=MESH,
        )

    def copy(slot, to, sem):
        return pltpu.make_async_remote_copy(
            src_ref=kbuf.at[slot], dst_ref=kbuf.at[slot], send_sem=ssem.at[sem], recv_sem=rsem.at[slot],
            device_id=(to, y), device_id_type=MESH,
        )

    def run(route):
        count = [0]

        def send(slot, *ways):
            for way in ways:
                copy(slot, ring[way], count[0]).start()
                count[0] += 1
            landed(slot)

        def arrive(slot):
            copy(slot, sibling, 0).wait_recv()

        route(send, arrive)
        return count[0]

    def z_first(send, arrive):
        zs = [z, z - 1, z + 1, z - 2, z + 2, z - 3, z + 3, z - 4]
        send(me, *(f"z{d}" for d in (1, 7, 2, 6, 3, 5, 4)), "x+", "x-", "s")
        for zz in zs[1:]:
            slot = pb(x, zz, core)
            arrive(slot)
            send(slot, "x+", "x-", "s")
        for i, zz in enumerate(zs):
            slot = pb(x - 1, zz, core)
            arrive(slot)
            send(slot, *(("x+", "s") if i % 2 == 0 else ("s",)))
            slot = pb(x + 1, zz, core)
            arrive(slot)
            send(slot, *(("x-", "s") if i % 2 == 1 else ("s",)))
        for zz in zs:
            slot = pb(x + 2, zz, core)
            arrive(slot)
            send(slot, "s")

    def x_first(send, arrive):
        send(me, "z1", "z7", "x+", "x-", "x2", "s")
        xs = [x, x - 1, x + 1, x + 2]
        for i in range(1, NX):
            slot = pb(xs[i], z, core)
            arrive(slot)
            send(slot, "z1", "z7", "s")
        for dist in range(1, 5):
            for i in range(NX):
                last_plus, last_minus = (4, 3) if i < 2 else (3, 4)
                if dist <= last_plus:
                    slot = pb(xs[i], z - dist, core)
                    arrive(slot)
                    send(slot, *(("z1", "s") if dist < last_plus else ("s",)))
                if dist <= last_minus:
                    slot = pb(xs[i], z + dist, core)
                    arrive(slot)
                    send(slot, *(("z7", "s") if dist < last_minus else ("s",)))

    for o in range(1, NY):
        q_copy(o).start()

    @pl.when(core == 0)
    def _():
        assert run(z_first) == 63

    @pl.when(core == 1)
    def _():
        assert run(x_first) == 63

    for o in range(1, NY):
        q_copy(o).wait()
    queries()

    @pl.loop(0, NX * NZ)
    def _(i):
        copy(2 * i + 1 - core, sibling, 0).wait_recv()
        landed(2 * i + 1 - core)

    @pl.loop(0, 63)
    def _(i):
        copy(me, sibling, i).wait_send()


def spread(slot, kbuf, kf_ref):
    for i in range(2):
        base = lax.div(slot, 4) * 512 + (lax.rem(slot, 4) * 2 + i) * 8
        for c in range(CELLS // 8):
            for h in range(2):
                to = pl.multiple_of(base + c * 64, 8) + h * NK
                kf_ref[pl.ds(to, 8), :] = kbuf[slot, i * CELLS + c * 8 : i * CELLS + c * 8 + 8, h * 128 : (h + 1) * 128].astype(f32)


def order_keys(kf_ref, kp_ref):
    @pl.loop(0, CELLS // 4)
    def _(i):
        for u in range(4):
            base = pl.multiple_of(lax.div(i, 2) * 64, 64) + lax.rem(i, 2) * 4 + u
            for h in range(2):
                for t in range(0, NT // 8, 2):
                    pair = [kf_ref[pl.ds(base + (t + j) * 512 + h * NK, 8, stride=8), :] for j in range(2)]
                    rows = pl.ds(pl.multiple_of((i * 4 + (0, 2, 1, 3)[u]) * NT + t * 8, 16), 16)
                    kp_ref[rows, h * 128 : (h + 1) * 128] = jnp.concatenate(pair, axis=0).astype(bf16)


def costs(qall, kp_ref, cost_ref):
    low = lax.broadcasted_iota(jnp.int32, (8, 128), 0) < 4

    @pl.loop(0, CELLS // 8)
    def _(jj):
        for u in range(2):
            j = jj * 2 + u
            r = pl.multiple_of(j * 512, 512)
            even = dot_nt(qall[0], kp_ref[pl.ds(r, 256), :])
            odd = dot_nt(qall[1], kp_ref[pl.ds(r + 256, 256), :])
            for v in range(NQ // 8):
                for h in range(2):
                    ev = even[v * 8 : v * 8 + 8, h * 128 : (h + 1) * 128]
                    od = odd[v * 8 : v * 8 + 8, h * 128 : (h + 1) * 128]
                    to = pl.multiple_of(v * 512 + j * 16 + h * 8, 8)
                    cost_ref[pl.ds(to, 8), :] = jnp.where(low, ev, od)
                    cost_ref[pl.ds(to + 256, 8), :] = jnp.where(low, od, ev)


def pipeline(mask_ref, wd_ref, bias_ref, gain_ref, smap_ref, w_ref, lse_ref, cost_ref, toks, nrms, ps, ms, after):
    lane = lax.broadcasted_iota(jnp.int32, (8, 128), 1)
    sub = lax.broadcasted_iota(jnp.int32, (8, 128), 0)
    lane64 = lax.broadcasted_iota(jnp.int32, (64, 128), 1)

    def sums(g, slot):
        nrm_ref, p_ref, m_ref = nrms[slot], ps[slot], ms[slot]
        b2 = lax.rem(g + 1, 2) * 2
        zero = jnp.zeros((16, 128), bf16)
        rows = []
        for lp in range(LAT):
            st = jnp.bitwise_xor(b2, lp)
            pa = p_ref[pl.ds(st, 16, stride=8), :].astype(bf16)
            pb = p_ref[pl.ds(st + 128, 16, stride=8), :].astype(bf16)
            rows += [jnp.concatenate([pa, zero], axis=1), jnp.concatenate([zero, pb], axis=1)]
        pst = jnp.concatenate(rows, axis=0)
        o = dot_nt(jnp.concatenate([nrm_ref[...], jnp.ones((16, 256), bf16)], axis=0), pst)
        acc = None
        for p in range(NP):
            ov = [o[p * 64 : (p + 1) * 64, v * 128 : (v + 1) * 128] for v in range(2)]
            own = lax.bitwise_and(lane64, 15) == p
            acc = ov if acc is None else [jnp.where(own, ov[v], acc[v]) for v in range(2)]
        d = o[NP * 64 : NP * 64 + 1, :]
        rd = 1.0 / d
        for v in range(2):
            vl = slice(v * 128, (v + 1) * 128)
            w_ref[pl.ds(pl.multiple_of(g * 64, 64), 64), vl] = acc[v] * rd[:, vl]
        lse_ref[pl.ds(pl.multiple_of(g * 8, 8), 8), :] = jnp.broadcast_to(m_ref[0:1, :] + jnp.log(d), (8, 256))
        yield

    def scores(g, slot):
        nrm_ref, p_ref, m_ref = nrms[slot], ps[slot], ms[slot]
        b2 = lax.rem(g, 2) * 2
        pos = lane - lax.bitwise_and(jnp.bitwise_xor(sub, b2), 3) * 32
        accm = jnp.zeros((8, 128), f32)
        for k in range(NP // 4):
            s3 = jnp.dot(smap_ref[...], nrm_ref[k * 256 : (k + 1) * 256, :], preferred_element_type=f32)
            for i in range(4):
                s = s3[24 * i : 24 * i + 8] + (s3[24 * i + 8 : 24 * i + 16] + s3[24 * i + 16 : 24 * i + 24])
                for h in range(2):
                    q = h * 16 + k * 4 + i
                    sq = s[:, h * 128 : (h + 1) * 128]
                    m = jnp.broadcast_to(jnp.max(sq, axis=1, keepdims=True), (8, 128))
                    p_ref[q * 8 : q * 8 + 8, :] = jnp.exp(sq - m)
                    accm = jnp.where(pos == q, m, accm)
            if k < NP // 4 - 1:
                yield
        m_ref[:, 0:128] = jnp.broadcast_to(jnp.sum(jnp.where(sub < 4, accm, 0.0), axis=0, keepdims=True), (8, 128))
        m_ref[:, 128:256] = jnp.broadcast_to(jnp.sum(jnp.where(sub < 4, 0.0, accm), axis=0, keepdims=True), (8, 128))
        yield

    def norms(slot):
        tok_ref, nrm_ref = toks[slot], nrms[slot]
        for i in range(NP):
            for h in range(2):
                hl = slice(h * 128, (h + 1) * 128)
                tok = tok_ref[i * 64 : (i + 1) * 64, hl] + bias_ref[:, hl]
                ss = jnp.sum(tok * tok, axis=0, keepdims=True)
                rstd = lax.rsqrt(ss * (1.0 / E) + 1e-5)
                nrm_ref[i * 64 : (i + 1) * 64, hl] = (tok * rstd * gain_ref[:, hl]).astype(bf16)
                yield

    def tokens(g, slot):
        q0 = jnp.minimum(g, NG - 1) * G
        for k in range(NP // 2):
            rows = []
            for i in range(2):
                xs = []
                for h in range(2):
                    q = h * 16 + k * 2 + i
                    base = pl.multiple_of((q0 + q // 4 * 4) * CELLS, 256) + q % 4
                    xq = cost_ref[pl.ds(base, CELLS, stride=4), :].astype(bf16)
                    mk = jnp.broadcast_to(mask_ref[pl.ds(q0 + q, 1), :].astype(f32), (CELLS, NT)).astype(bf16)
                    xs.append(xq * mk)
                xx = jnp.concatenate(xs, axis=1)
                rows += [xx, xx]
            toks[slot][k * 128 : (k + 1) * 128, :] = jnp.dot(
                wd_ref[k % 4 // 2], jnp.concatenate(rows, axis=0), preferred_element_type=f32
            )
            yield

    def block(g, u, order):
        steps = {"w": sums(g, u), "s": scores(g, (u + 1) % 3), "n": norms((u + 2) % 3), "t": tokens(g, u)}
        for step in order:
            next(steps[step])

    block(0, 0, "t" * 8)
    block(1, 1, "tnnnn" * 8)
    block(2, 2, "snn" * 4 + "tnnn" * 8)

    @pl.loop(1, 7)
    def _(it):
        for u in range(3):
            g = it * 3 + u

            @pl.when(g < NG + 1)
            def _():
                block(g, u, "w" + "n" * 16 + "snn" * 4 + "tn" * 8)
                after(g)

    block(NG + 1, (NG + 1) % 3, "w" + "ssss")
    block(NG + 2, (NG + 2) % 3, "w")
    after(NG + 2)


def split(a, n):
    parts = []
    for _ in range(n):
        parts.append(a.astype(bf16).astype(f32))
        a = a - parts[-1]
    return parts


def parameters(weight_ref, pbias_ref, pgain_ref, latq_ref, key_ref, wd_ref, bias_ref, gain_ref, smap_ref):
    weight = weight_ref[...].astype(f32)
    even = lax.rem(lax.broadcasted_iota(jnp.int32, (CELLS, E), 0), 2) == 0
    swapped = jnp.where(even, pltpu.roll(weight, CELLS - 1, 0), pltpu.roll(weight, 1, 0))
    zero = jnp.zeros((E, 128), f32)
    for i, form in enumerate((weight, swapped)):
        form = form.T
        centred = (form - jnp.mean(form, axis=0, keepdims=True)) / math.sqrt(CH)
        parts = jnp.concatenate(split(centred, 2), axis=1)
        wd_ref[i] = jnp.concatenate(
            [jnp.concatenate([parts, zero], axis=1), jnp.concatenate([zero, parts], axis=1)], axis=0
        ).astype(bf16)
    bias = pbias_ref[...]
    bias = bias - jnp.mean(bias, axis=1, keepdims=True)
    for source, ref in ((bias, bias_ref), (pgain_ref[...], gain_ref)):
        column = jnp.broadcast_to(source, (128, E)).T
        ref[:, 0:128] = column
        ref[:, 128:256] = column
    score_map = lax.dot_general(
        latq_ref[...], key_ref[...].astype(f32), (((1,), (1,)), ((), ())),
        precision=lax.Precision.HIGHEST, preferred_element_type=f32,
    ) / math.sqrt(LD)
    parts = jnp.concatenate(split(score_map, 3), axis=0)
    zero = jnp.zeros_like(parts)
    smap_ref[...] = jnp.concatenate(
        [jnp.concatenate([parts if i == j else zero for j in range(4)], axis=1) for i in range(4)], axis=0
    ).astype(bf16)


def kernel(
    q_ref, k_ref, mask_ref, weight_ref, pbias_ref, pgain_ref, latq_ref, key_ref, value_ref, out_ref,
    kbuf, qbuf, kf_ref, kp_ref, qall, cost_ref, toks, nrms, ps, ms, w_ref, lse_ref, wd_ref, bias_ref, gain_ref, smap_ref,
    sbuf, sst, rbuf, rst, ssem, rsem, qssem, qrsem, dssem, drsem, tssem, trsem,
):
    me = lax.axis_index("pb")
    y = lax.axis_index("ka")
    def prepare():
        parameters(weight_ref, pbias_ref, pgain_ref, latq_ref, key_ref, wd_ref, bias_ref, gain_ref, smap_ref)

    def queries():
        rows = jnp.concatenate([qbuf[i] for i in range(NY)], axis=0).astype(f32).T
        qall[0] = rows.astype(bf16)
        qall[1] = pltpu.roll(rows.reshape(NQ // 8, 8, CH), 4, 1).reshape(NQ, CH).astype(bf16)

    def landed(slot):
        spread(slot, kbuf, kf_ref)

    gather(me, y, k_ref, q_ref, kbuf, qbuf, ssem, rsem, qssem, qrsem, prepare, queries, landed)
    order_keys(kf_ref, kp_ref)
    costs(qall, kp_ref, cost_ref)
    lane64 = lax.broadcasted_iota(jnp.int32, (64, 128), 1)
    lane8 = lax.broadcasted_iota(jnp.int32, (8, 128), 1)

    def copies(k, o):
        to = lax.rem(y + o, NY)
        rows = pl.ds(pl.multiple_of(k * 128, 128), 128)
        st = pl.ds(pl.multiple_of(k * 16, 16), 16)
        return (
            pltpu.make_async_remote_copy(
                src_ref=sbuf.at[to, rows], dst_ref=rbuf.at[o - 1, rows], send_sem=dssem.at[o - 1, k],
                recv_sem=drsem.at[o - 1, k], device_id=(me, to), device_id_type=MESH,
            ),
            pltpu.make_async_remote_copy(
                src_ref=sst.at[to, st], dst_ref=rst.at[o - 1, st], send_sem=tssem.at[o - 1, k],
                recv_sem=trsem.at[o - 1, k], device_id=(me, to), device_id_type=MESH,
            ),
        )

    def send_chunk(k):
        for blk in range(2):
            ga = k * GPC + blk * 2 + 3
            for v in range(2):
                vl = slice(v * 128, (v + 1) * 128)
                wa = w_ref[pl.ds(pl.multiple_of(ga * 64, 64), 64), vl]
                wb = w_ref[pl.ds(pl.multiple_of(ga * 64 + 64, 64), 64), vl]
                la = lse_ref[pl.ds(pl.multiple_of(ga * 8, 8), 8), vl]
                lb = lse_ref[pl.ds(pl.multiple_of(ga * 8 + 8, 8), 8), vl]
                rows = pl.ds(pl.multiple_of(k * 128 + blk * 64, 64), 64)
                st = pl.ds(pl.multiple_of(k * 16 + blk * 8, 8), 8)
                sbuf[2 * v, rows, :] = jnp.where(lane64 < 64, wa, wb).astype(bf16)
                sbuf[2 * v + 1, rows, :] = jnp.where(lane64 < 64, wb, wa).astype(bf16)
                sst[2 * v, st, :] = jnp.where(lane8 < 64, la, lb)
                sst[2 * v + 1, st, :] = jnp.where(lane8 < 64, lb, la)
        for o in range(1, NY):
            for c in copies(k, o):
                c.start()

    def combine_chunk(k):
        for o in range(1, NY):
            for c in copies(k, o):
                c.wait_recv()
        odd = lax.rem(y, 2)
        for blk in range(2):
            rows = pl.ds(pl.multiple_of(k * 128 + blk * 64, 64), 64)
            st = pl.ds(pl.multiple_of(k * 16 + blk * 8, 8), 8)
            lses = [sst[y, st, :]] + [rst[o, st, :] for o in range(NY - 1)]
            vals = [sbuf[y, rows, :]] + [rbuf[o, rows, :] for o in range(NY - 1)]
            top = jnp.maximum(jnp.maximum(lses[0], lses[1]), jnp.maximum(lses[2], lses[3]))
            facs = [jnp.exp(a - top) for a in lses]
            inv = 1.0 / (facs[0] + facs[1] + facs[2] + facs[3])
            pooled = sum(v.astype(f32) * (a * inv)[0:1, :] for v, a in zip(vals, facs))
            res = lax.dot_general(
                pooled.astype(bf16), value_ref[...], (((0,), (0,)), ((), ())), preferred_element_type=f32
            ).astype(bf16)
            for half in range(2):
                off = odd * 32 if half == 0 else (1 - odd) * 32
                orow = pl.ds(pl.multiple_of(k * 128 + blk * 64 + off, 32), 32)
                for l in range(2):
                    r = (half * 2 + l) * 32
                    out_ref[orow, l * 128 : (l + 1) * 128] = res[r : r + 32, :]

    def after(g):
        @pl.when(jnp.logical_and(lax.rem(g, GPC) == 2, g > 3))
        def _():
            k = lax.div(g - 3, GPC)
            send_chunk(k)

    pipeline(mask_ref, wd_ref, bias_ref, gain_ref, smap_ref, w_ref, lse_ref, cost_ref, toks, nrms, ps, ms, after)

    @pl.loop(0, NCH)
    def _(k):
        combine_chunk(k)

    @pl.loop(0, NCH)
    def _(k):
        for o in range(1, NY):
            for c in copies(k, o):
                c.wait_send()


def body(
    query_features, key_features, patch_weight, patch_bias, norm_gain, latent_queries, key_weight, value_weight, keep_mask
):
    vmem = pl.BlockSpec(memory_space=pltpu.VMEM)
    dma = pltpu.SemaphoreType.DMA
    out = pl.pallas_call(
        kernel,
        out_shape=jax.ShapeDtypeStruct((NQ, 2 * LD), bf16),
        in_specs=[vmem] * 9,
        out_specs=vmem,
        scratch_shapes=[
            pltpu.VMEM((2 * NX * NZ, 128, CH), bf16),
            pltpu.VMEM((NY, CH // NY, NQ), bf16),
            pltpu.VMEM((2 * NK, 128), f32),
            pltpu.VMEM((NK, CH), bf16),
            pltpu.VMEM((2, NQ, CH), bf16),
            pltpu.VMEM((CELLS * NQ, NT), f32),
            [pltpu.VMEM((NP * E, 256), f32)] * 3,
            [pltpu.VMEM((NP * E, 256), bf16)] * 3,
            [pltpu.VMEM((G * LAT, NT), f32)] * 3,
            [pltpu.VMEM((8, 256), f32)] * 3,
            pltpu.VMEM(((NG + 3) * E, 256), f32),
            pltpu.VMEM(((NG + 3) * 8, 256), f32),
            pltpu.VMEM((2, 2 * E, 256), bf16),
            pltpu.VMEM((E, 256), f32),
            pltpu.VMEM((E, 256), f32),
            pltpu.VMEM((96, 256), bf16),
            pltpu.VMEM((NY, NQ, 128), bf16),
            pltpu.VMEM((NY, NCH * 16, 128), f32),
            pltpu.VMEM((NY - 1, NQ, 128), bf16),
            pltpu.VMEM((NY - 1, NCH * 16, 128), f32),
            dma((64,)),
            dma((64,)),
            dma((NY - 1,)),
            dma((NY - 1,)),
            dma((NY - 1, NCH)),
            dma((NY - 1, NCH)),
            dma((NY - 1, NCH)),
            dma((NY - 1, NCH)),
        ],
        compiler_params=pltpu.CompilerParams(
            collective_id=0, has_side_effects=True, vmem_limit_bytes=60 * 1024 * 1024
        ),
    )(
        query_features.T, key_features, keep_mask, patch_weight, patch_bias.reshape(1, E), norm_gain.reshape(1, E),
        latent_queries, key_weight, value_weight,
    )
    return out.reshape(NQ, 2, LD)


def solution(mesh):
    placed = (P("pb", "ka"), P(("ka", "pb"), None), P(), P(), P(), P(), P(), P(), P("pb", "ka"))
    return jax.shard_map(
        body, mesh=mesh, in_specs=placed, out_specs=P("pb", "ka", None), check_vma=False
    )
```

```python
import math

import jax
import jax.numpy as jnp
from jax import lax
from jax.experimental import pallas as pl
from jax.experimental.pallas import tpu as pltpu
from jax.sharding import PartitionSpec as P

f32 = jnp.float32
bf16 = jnp.bfloat16
MESH = pl.DeviceIdType.MESH

NX, NZ, NY = 4, 8, 4
NQ, NT, CELLS, CH, E, LAT, LD = 640, 128, 64, 256, 64, 8, 128
NK = NT * CELLS
G = 32
NG = NQ // G
NP = G // 2
CHUNK = 128
NCH = NQ // CHUNK
GPC = CHUNK // G


def dot_nt(a, b):
    return lax.dot_general(a, b, (((1,), (1,)), ((), ())), preferred_element_type=f32)


def gather(me, y, k_ref, q_ref, kbuf, qbuf, ssem, rsem, qssem, qrsem, prepare, queries, landed):
    core = lax.rem(me, 2)
    z = lax.rem(lax.div(me, 2), NZ)
    x = lax.div(me, 2 * NZ)

    def pb(xx, zz, cc):
        return (lax.rem(xx + NX, NX) * NZ + lax.rem(zz + NZ, NZ)) * 2 + cc

    sibling = pb(x, z, 1 - core)
    ring = {f"z{d}": pb(x, z + d, core) for d in range(1, NZ)}
    ring.update({"x+": pb(x + 1, z, core), "x-": pb(x - 1, z, core), "x2": pb(x + 2, z, core), "s": sibling})

    barrier = pltpu.get_barrier_semaphore()
    for other in ring.values():
        pl.semaphore_signal(barrier, inc=1, device_id=(other, y), device_id_type=MESH)
    for o in range(1, NY):
        pl.semaphore_signal(barrier, inc=1, device_id=(me, lax.rem(y + o, NY)), device_id_type=MESH)
    kbuf[me] = k_ref[...]
    qbuf[y] = q_ref[...]
    prepare()
    pl.semaphore_wait(barrier, len(ring) + NY - 1)

    def q_copy(o):
        return pltpu.make_async_remote_copy(
            src_ref=qbuf.at[y], dst_ref=qbuf.at[y], send_sem=qssem.at[o - 1], recv_sem=qrsem.at[o - 1],
            device_id=(me, lax.rem(y + o, NY)), device_id_type=MESH,
        )

    def copy(slot, to, sem):
        return pltpu.make_async_remote_copy(
            src_ref=kbuf.at[slot], dst_ref=kbuf.at[slot], send_sem=ssem.at[sem], recv_sem=rsem.at[slot],
            device_id=(to, y), device_id_type=MESH,
        )

    def run(route):
        count = [0]

        def send(slot, *ways):
            for way in ways:
                copy(slot, ring[way], count[0]).start()
                count[0] += 1
            landed(slot)

        def arrive(slot):
            copy(slot, sibling, 0).wait_recv()

        route(send, arrive)
        return count[0]

    def z_first(send, arrive):
        zs = [z, z - 1, z + 1, z - 2, z + 2, z - 3, z + 3, z - 4]
        send(me, *(f"z{d}" for d in (1, 7, 2, 6, 3, 5, 4)), "x+", "x-", "s")
        for zz in zs[1:]:
            slot = pb(x, zz, core)
            arrive(slot)
            send(slot, "x+", "x-", "s")
        for i, zz in enumerate(zs):
            slot = pb(x - 1, zz, core)
            arrive(slot)
            send(slot, *(("x+", "s") if i % 2 == 0 else ("s",)))
            slot = pb(x + 1, zz, core)
            arrive(slot)
            send(slot, *(("x-", "s") if i % 2 == 1 else ("s",)))
        for zz in zs:
            slot = pb(x + 2, zz, core)
            arrive(slot)
            send(slot, "s")

    def x_first(send, arrive):
        send(me, "z1", "z7", "x+", "x-", "x2", "s")
        xs = [x, x - 1, x + 1, x + 2]
        for i in range(1, NX):
            slot = pb(xs[i], z, core)
            arrive(slot)
            send(slot, "z1", "z7", "s")
        for dist in range(1, 5):
            for i in range(NX):
                last_plus, last_minus = (4, 3) if i < 2 else (3, 4)
                if dist <= last_plus:
                    slot = pb(xs[i], z - dist, core)
                    arrive(slot)
                    send(slot, *(("z1", "s") if dist < last_plus else ("s",)))
                if dist <= last_minus:
                    slot = pb(xs[i], z + dist, core)
                    arrive(slot)
                    send(slot, *(("z7", "s") if dist < last_minus else ("s",)))

    for o in range(1, NY):
        q_copy(o).start()

    @pl.when(core == 0)
    def _():
        assert run(z_first) == 63

    @pl.when(core == 1)
    def _():
        assert run(x_first) == 63

    for o in range(1, NY):
        q_copy(o).wait()
    queries()

    @pl.loop(0, NX * NZ)
    def _(i):
        copy(2 * i + 1 - core, sibling, 0).wait_recv()
        landed(2 * i + 1 - core)

    def sent():
        @pl.loop(0, 63)
        def _(i):
            copy(me, sibling, i).wait_send()

    return sent


def spread(slot, kbuf, kf_ref):
    for i in range(2):
        base = lax.div(slot, 4) * 512 + (lax.rem(slot, 4) * 2 + i) * 8
        for c in range(CELLS // 8):
            for h in range(2):
                to = pl.multiple_of(base + c * 64, 8) + h * NK
                kf_ref[pl.ds(to, 8), :] = kbuf[slot, i * CELLS + c * 8 : i * CELLS + c * 8 + 8, h * 128 : (h + 1) * 128].astype(f32)


def order_keys(kf_ref, kp_ref):
    @pl.loop(0, CELLS // 4)
    def _(i):
        for u in range(4):
            base = pl.multiple_of(lax.div(i, 2) * 64, 64) + lax.rem(i, 2) * 4 + u
            for h in range(2):
                for t in range(0, NT // 8, 2):
                    pair = [kf_ref[pl.ds(base + (t + j) * 512 + h * NK, 8, stride=8), :] for j in range(2)]
                    rows = pl.ds(pl.multiple_of((i * 4 + (0, 2, 1, 3)[u]) * NT + t * 8, 16), 16)
                    kp_ref[rows, h * 128 : (h + 1) * 128] = jnp.concatenate(pair, axis=0).astype(bf16)


def costs(qall, kp_ref, cost_ref):
    low = lax.broadcasted_iota(jnp.int32, (8, 128), 0) < 4

    @pl.loop(0, CELLS // 8)
    def _(jj):
        for u in range(2):
            j = jj * 2 + u
            r = pl.multiple_of(j * 512, 512)
            even = dot_nt(qall[0], kp_ref[pl.ds(r, 256), :])
            odd = dot_nt(qall[1], kp_ref[pl.ds(r + 256, 256), :])
            for v in range(NQ // 8):
                for h in range(2):
                    ev = even[v * 8 : v * 8 + 8, h * 128 : (h + 1) * 128]
                    od = odd[v * 8 : v * 8 + 8, h * 128 : (h + 1) * 128]
                    to = pl.multiple_of(v * 512 + j * 16 + h * 8, 8)
                    cost_ref[pl.ds(to, 8), :] = jnp.where(low, ev, od)
                    cost_ref[pl.ds(to + 256, 8), :] = jnp.where(low, od, ev)


def pipeline(mask_ref, wd_ref, bias_ref, gain_ref, smap_ref, w_ref, lse_ref, cost_ref, toks, nrms, ps, ms, after):
    lane = lax.broadcasted_iota(jnp.int32, (8, 128), 1)
    sub = lax.broadcasted_iota(jnp.int32, (8, 128), 0)
    lane64 = lax.broadcasted_iota(jnp.int32, (64, 128), 1)

    def sums(g, slot):
        nrm_ref, p_ref, m_ref = nrms[slot], ps[slot], ms[slot]
        b4 = lax.rem(g + 1, 2) * 4
        zero = jnp.zeros((8, 128), f32)
        for hh in range(2):
            rows = []
            for lp in range(LAT):
                st = jnp.bitwise_xor(b4, lp ^ (2 * hh)) + hh * 128
                pa = p_ref[pl.ds(st, 8, stride=8), :]
                pb = p_ref[pl.ds(st + 64, 8, stride=8), :]
                left, right = jnp.concatenate([pa, zero], axis=0), jnp.concatenate([zero, pb], axis=0)
                rows.append(jnp.concatenate([left.astype(bf16), right.astype(bf16)], axis=1))
            lhs = jnp.concatenate([nrm_ref[hh * 512 : hh * 512 + 512, :], jnp.ones((16, 256), bf16)], axis=0)
            o = dot_nt(lhs, jnp.concatenate(rows, axis=0))
            acc = o[0:64, :]
            for p in range(1, 8):
                acc = jnp.where(lax.bitwise_and(lane64, 7) == p, o[p * 64 : (p + 1) * 64, :], acc)
            d = o[512:513, :]
            vl = slice(hh * 128, (hh + 1) * 128)
            w_ref[pl.ds(pl.multiple_of(g * 64, 64), 64), vl] = acc * (1.0 / d)
            lse_ref[pl.ds(pl.multiple_of(g * 8, 8), 8), vl] = jnp.broadcast_to(m_ref[0:1, vl] + jnp.log(d), (8, 128))
            yield

    def scores(g, slot):
        nrm_ref, p_ref, m_ref = nrms[slot], ps[slot], ms[slot]
        b4 = lax.rem(g, 2) * 4
        pos = [lane - jnp.bitwise_xor(sub, b4 + 2 * hh) * 16 for hh in range(2)]
        accm = [jnp.zeros((8, 128), f32)] * 2
        for k in range(NP // 4):
            s3 = jnp.dot(smap_ref[...], nrm_ref[k * 256 : (k + 1) * 256, :], preferred_element_type=f32)
            for i in range(4):
                s = s3[24 * i : 24 * i + 8] + (s3[24 * i + 8 : 24 * i + 16] + s3[24 * i + 16 : 24 * i + 24])
                for h in range(2):
                    hh, p = divmod(k * 4 + i, 8)
                    q = hh * 16 + h * 8 + p
                    sq = s[:, h * 128 : (h + 1) * 128]
                    m = jnp.broadcast_to(jnp.max(sq, axis=1, keepdims=True), (8, 128))
                    p_ref[q * 8 : q * 8 + 8, :] = jnp.exp(sq - m)
                    accm[hh] = jnp.where(pos[hh] == h * 8 + p, m, accm[hh])
            if k < NP // 4 - 1:
                yield
        for hh in range(2):
            m_ref[:, hh * 128 : (hh + 1) * 128] = jnp.broadcast_to(jnp.sum(accm[hh], axis=0, keepdims=True), (8, 128))
        yield

    def norms(slot):
        tok_ref, nrm_ref = toks[slot], nrms[slot]
        for i in range(NP):
            for h in range(2):
                hl = slice(h * 128, (h + 1) * 128)
                tok = tok_ref[i * 64 : (i + 1) * 64, hl] + bias_ref[:, hl]
                ss = jnp.sum(tok * tok, axis=0, keepdims=True)
                rstd = lax.rsqrt(ss * (1.0 / E) + 1e-5)
                nrm_ref[i * 64 : (i + 1) * 64, hl] = (tok * rstd * gain_ref[:, hl]).astype(bf16)
                yield

    def tokens(g, slot):
        q0 = jnp.minimum(g, NG - 1) * G
        for k in range(NP // 2):
            rows = []
            for i in range(2):
                xs = []
                for h in range(2):
                    q = (k * 2 + i) // 8 * 16 + h * 8 + (k * 2 + i) % 8
                    base = pl.multiple_of((q0 + q // 4 * 4) * CELLS, 256) + q % 4
                    xq = cost_ref[pl.ds(base, CELLS, stride=4), :].astype(bf16)
                    mk = jnp.broadcast_to(mask_ref[pl.ds(q0 + q, 1), :].astype(f32), (CELLS, NT)).astype(bf16)
                    xs.append(xq * mk)
                xx = jnp.concatenate(xs, axis=1)
                rows += [xx, xx]
            toks[slot][k * 128 : (k + 1) * 128, :] = jnp.dot(
                wd_ref[k % 4 // 2], jnp.concatenate(rows, axis=0), preferred_element_type=f32
            )
            yield

    def block(g, u, order):
        steps = {"w": sums(g, u), "s": scores(g, (u + 1) % 3), "n": norms((u + 2) % 3), "t": tokens(g, u)}
        for step in order:
            next(steps[step])

    block(0, 0, "t" * 8)
    block(1, 1, "tnnnn" * 8)
    block(2, 2, "snn" * 4 + "tnnn" * 8)

    @pl.loop(1, 7)
    def _(it):
        for u in range(3):
            g = it * 3 + u

            @pl.when(g < NG + 1)
            def _():
                block(g, u, "wnnnnnnnn" * 2 + "snn" * 4 + "tn" * 8)
                after(g)

    block(NG + 1, (NG + 1) % 3, "ww" + "ssss")
    block(NG + 2, (NG + 2) % 3, "ww")
    after(NG + 2)


def split(a, n):
    parts = []
    for _ in range(n):
        parts.append(a.astype(bf16).astype(f32))
        a = a - parts[-1]
    return parts


def parameters(weight_ref, pbias_ref, pgain_ref, latq_ref, key_ref, wd_ref, bias_ref, gain_ref, smap_ref):
    weight = weight_ref[...].astype(f32)
    even = lax.rem(lax.broadcasted_iota(jnp.int32, (CELLS, E), 0), 2) == 0
    swapped = jnp.where(even, pltpu.roll(weight, CELLS - 1, 0), pltpu.roll(weight, 1, 0))
    zero = jnp.zeros((E, 128), f32)
    for i, form in enumerate((weight, swapped)):
        form = form.T
        centred = (form - jnp.mean(form, axis=0, keepdims=True)) / math.sqrt(CH)
        parts = jnp.concatenate(split(centred, 2), axis=1)
        wd_ref[i] = jnp.concatenate(
            [jnp.concatenate([parts, zero], axis=1), jnp.concatenate([zero, parts], axis=1)], axis=0
        ).astype(bf16)
    bias = pbias_ref[...]
    bias = bias - jnp.mean(bias, axis=1, keepdims=True)
    for source, ref in ((bias, bias_ref), (pgain_ref[...], gain_ref)):
        column = jnp.broadcast_to(source, (128, E)).T
        ref[:, 0:128] = column
        ref[:, 128:256] = column
    score_map = lax.dot_general(
        latq_ref[...], key_ref[...].astype(f32), (((1,), (1,)), ((), ())),
        precision=lax.Precision.HIGHEST, preferred_element_type=f32,
    ) / math.sqrt(LD)
    parts = jnp.concatenate(split(score_map, 3), axis=0)
    zero = jnp.zeros_like(parts)
    smap_ref[...] = jnp.concatenate(
        [jnp.concatenate([parts if i == j else zero for j in range(4)], axis=1) for i in range(4)], axis=0
    ).astype(bf16)


def kernel(
    q_ref, k_ref, mask_ref, weight_ref, pbias_ref, pgain_ref, latq_ref, key_ref, value_ref, out_ref,
    kbuf, qbuf, kf_ref, kp_ref, qall, cost_ref, toks, nrms, ps, ms, w_ref, lse_ref, wd_ref, bias_ref, gain_ref, smap_ref,
    sbuf, sst, rbuf, rst, ssem, rsem, qssem, qrsem, dssem, drsem, tssem, trsem,
):
    me = lax.axis_index("pb")
    y = lax.axis_index("ka")
    def prepare():
        parameters(weight_ref, pbias_ref, pgain_ref, latq_ref, key_ref, wd_ref, bias_ref, gain_ref, smap_ref)

    def queries():
        rows = jnp.concatenate([qbuf[i] for i in range(NY)], axis=0).astype(f32).T
        qall[0] = rows.astype(bf16)
        qall[1] = pltpu.roll(rows.reshape(NQ // 8, 8, CH), 4, 1).reshape(NQ, CH).astype(bf16)

    def landed(slot):
        spread(slot, kbuf, kf_ref)

    sent = gather(me, y, k_ref, q_ref, kbuf, qbuf, ssem, rsem, qssem, qrsem, prepare, queries, landed)
    order_keys(kf_ref, kp_ref)
    costs(qall, kp_ref, cost_ref)
    lane64 = lax.broadcasted_iota(jnp.int32, (64, 128), 1)
    lane8 = lax.broadcasted_iota(jnp.int32, (8, 128), 1)

    def copies(k, o):
        to = lax.rem(y + o, NY)
        rows = pl.ds(pl.multiple_of(k * 128, 128), 128)
        st = pl.ds(pl.multiple_of(k * 16, 16), 16)
        return (
            pltpu.make_async_remote_copy(
                src_ref=sbuf.at[to, rows], dst_ref=rbuf.at[o - 1, rows], send_sem=dssem.at[o - 1, k],
                recv_sem=drsem.at[o - 1, k], device_id=(me, to), device_id_type=MESH,
            ),
            pltpu.make_async_remote_copy(
                src_ref=sst.at[to, st], dst_ref=rst.at[o - 1, st], send_sem=tssem.at[o - 1, k],
                recv_sem=trsem.at[o - 1, k], device_id=(me, to), device_id_type=MESH,
            ),
        )

    def quarters(lane, a):
        return jnp.where(lane < 64, jnp.where(lane < 32, a[0], a[1]), jnp.where(lane < 96, a[2], a[3]))

    def send_chunk(k):
        for blk in range(2):
            ga = k * GPC + blk * 2 + 3
            rows = pl.ds(pl.multiple_of(k * 128 + blk * 64, 64), 64)
            st = pl.ds(pl.multiple_of(k * 16 + blk * 8, 8), 8)
            wr = [pl.ds(pl.multiple_of((ga + i) * 64, 64), 64) for i in range(2)]
            lr = [pl.ds(pl.multiple_of((ga + i) * 8, 8), 8) for i in range(2)]
            vl = [slice(hh * 128, (hh + 1) * 128) for hh in range(2)]
            ws = [w_ref[wr[hg // 2], vl[hg % 2]] for hg in range(4)]
            ls = [lse_ref[lr[hg // 2], vl[hg % 2]] for hg in range(4)]
            for j in range(NY):
                sbuf[j, rows, :] = quarters(lane64, [ws[j ^ i] for i in range(4)]).astype(bf16)
                sst[j, st, :] = quarters(lane8, [ls[j ^ i] for i in range(4)])
        for o in range(1, NY):
            for c in copies(k, o):
                c.start()

    def combine_chunk(k):
        for o in range(1, NY):
            for c in copies(k, o):
                c.wait_recv()
        for blk in range(2):
            rows = pl.ds(pl.multiple_of(k * 128 + blk * 64, 64), 64)
            st = pl.ds(pl.multiple_of(k * 16 + blk * 8, 8), 8)
            lses = [sst[y, st, :]] + [rst[o, st, :] for o in range(NY - 1)]
            vals = [sbuf[y, rows, :]] + [rbuf[o, rows, :] for o in range(NY - 1)]
            top = jnp.maximum(jnp.maximum(lses[0], lses[1]), jnp.maximum(lses[2], lses[3]))
            facs = [jnp.exp(a - top) for a in lses]
            inv = 1.0 / (facs[0] + facs[1] + facs[2] + facs[3])
            pooled = sum(v.astype(f32) * (a * inv)[0:1, :] for v, a in zip(vals, facs))
            res = lax.dot_general(
                pooled.astype(bf16), value_ref[...], (((0,), (0,)), ((), ())), preferred_element_type=f32
            ).astype(bf16)
            for i in range(4):
                off = jnp.bitwise_xor(y, i) * 16
                orow = pl.ds(pl.multiple_of(k * 128 + blk * 64 + off, 16), 16)
                for l in range(2):
                    r = i * 32 + l * 16
                    out_ref[orow, l * 128 : (l + 1) * 128] = res[r : r + 16, :]

    def after(g):
        @pl.when(jnp.logical_and(lax.rem(g, GPC) == 2, g > 3))
        def _():
            k = lax.div(g - 3, GPC)
            send_chunk(k)

    pipeline(mask_ref, wd_ref, bias_ref, gain_ref, smap_ref, w_ref, lse_ref, cost_ref, toks, nrms, ps, ms, after)

    def chunk_sent(k):
        for o in range(1, NY):
            for c in copies(k, o):
                c.wait_send()

    sent()
    pl.loop(0, NCH - 1)(chunk_sent)
    pl.loop(0, NCH)(combine_chunk)
    chunk_sent(NCH - 1)


def body(
    query_features, key_features, patch_weight, patch_bias, norm_gain, latent_queries, key_weight, value_weight, keep_mask
):
    vmem = pl.BlockSpec(memory_space=pltpu.VMEM)
    dma = pltpu.SemaphoreType.DMA
    out = pl.pallas_call(
        kernel,
        out_shape=jax.ShapeDtypeStruct((NQ, 2 * LD), bf16),
        in_specs=[vmem] * 9,
        out_specs=vmem,
        scratch_shapes=[
            pltpu.VMEM((2 * NX * NZ, 128, CH), bf16),
            pltpu.VMEM((NY, CH // NY, NQ), bf16),
            pltpu.VMEM((2 * NK, 128), f32),
            pltpu.VMEM((NK, CH), bf16),
            pltpu.VMEM((2, NQ, CH), bf16),
            pltpu.VMEM((CELLS * NQ, NT), f32),
            [pltpu.VMEM((NP * E, 256), f32)] * 3,
            [pltpu.VMEM((NP * E, 256), bf16)] * 3,
            [pltpu.VMEM((G * LAT, NT), f32)] * 3,
            [pltpu.VMEM((8, 256), f32)] * 3,
            pltpu.VMEM(((NG + 3) * E, 256), f32),
            pltpu.VMEM(((NG + 3) * 8, 256), f32),
            pltpu.VMEM((2, 2 * E, 256), bf16),
            pltpu.VMEM((E, 256), f32),
            pltpu.VMEM((E, 256), f32),
            pltpu.VMEM((96, 256), bf16),
            pltpu.VMEM((NY, NQ, 128), bf16),
            pltpu.VMEM((NY, NCH * 16, 128), f32),
            pltpu.VMEM((NY - 1, NQ, 128), bf16),
            pltpu.VMEM((NY - 1, NCH * 16, 128), f32),
            dma((64,)),
            dma((64,)),
            dma((NY - 1,)),
            dma((NY - 1,)),
            dma((NY - 1, NCH)),
            dma((NY - 1, NCH)),
            dma((NY - 1, NCH)),
            dma((NY - 1, NCH)),
        ],
        compiler_params=pltpu.CompilerParams(
            collective_id=0, has_side_effects=True, vmem_limit_bytes=60 * 1024 * 1024
        ),
    )(
        query_features.T, key_features, keep_mask, patch_weight, patch_bias.reshape(1, E), norm_gain.reshape(1, E),
        latent_queries, key_weight, value_weight,
    )
    return out.reshape(NQ, 2, LD)


def solution(mesh):
    placed = (P("pb", "ka"), P(("ka", "pb"), None), P(), P(), P(), P(), P(), P(), P("pb", "ka"))
    return jax.shard_map(
        body, mesh=mesh, in_specs=placed, out_specs=P("pb", "ka", None), check_vma=False
    )
```

```python
import math

import jax
import jax.numpy as jnp
from jax import lax
from jax.experimental import pallas as pl
from jax.experimental.pallas import tpu as pltpu
from jax.sharding import PartitionSpec as P

f32 = jnp.float32
bf16 = jnp.bfloat16
MESH = pl.DeviceIdType.MESH

NX, NZ, NY = 4, 8, 4
NQ, NT, CELLS, CH, E, LAT, LD = 640, 128, 64, 256, 64, 8, 128
NK = NT * CELLS
G = 32
NG = NQ // G
NP = G // 2
CHUNK = 128
NCH = NQ // CHUNK
GPC = CHUNK // G


def dot_nt(a, b):
    return lax.dot_general(a, b, (((1,), (1,)), ((), ())), preferred_element_type=f32)


def gather(me, y, k_ref, q_ref, kbuf, qbuf, ssem, rsem, qssem, qrsem, prepare, queries, landed):
    core = lax.rem(me, 2)
    z = lax.rem(lax.div(me, 2), NZ)
    x = lax.div(me, 2 * NZ)

    def pb(xx, zz, cc):
        return (lax.rem(xx + NX, NX) * NZ + lax.rem(zz + NZ, NZ)) * 2 + cc

    sibling = pb(x, z, 1 - core)
    ring = {f"z{d}": pb(x, z + d, core) for d in range(1, NZ)}
    ring.update({"x+": pb(x + 1, z, core), "x-": pb(x - 1, z, core), "x2": pb(x + 2, z, core), "s": sibling})

    barrier = pltpu.get_barrier_semaphore()
    for other in ring.values():
        pl.semaphore_signal(barrier, inc=1, device_id=(other, y), device_id_type=MESH)
    for o in range(1, NY):
        pl.semaphore_signal(barrier, inc=1, device_id=(me, lax.rem(y + o, NY)), device_id_type=MESH)
    kbuf[me] = k_ref[...]
    qbuf[y] = q_ref[...]
    prepare()
    pl.semaphore_wait(barrier, len(ring) + NY - 1)

    def q_copy(o):
        return pltpu.make_async_remote_copy(
            src_ref=qbuf.at[y], dst_ref=qbuf.at[y], send_sem=qssem.at[o - 1], recv_sem=qrsem.at[o - 1],
            device_id=(me, lax.rem(y + o, NY)), device_id_type=MESH,
        )

    def copy(slot, to, sem):
        return pltpu.make_async_remote_copy(
            src_ref=kbuf.at[slot], dst_ref=kbuf.at[slot], send_sem=ssem.at[sem], recv_sem=rsem.at[slot],
            device_id=(to, y), device_id_type=MESH,
        )

    def run(route):
        count = [0]

        def send(slot, *ways):
            for way in ways:
                copy(slot, ring[way], count[0]).start()
                count[0] += 1
            landed(slot)

        def arrive(slot):
            copy(slot, sibling, 0).wait_recv()

        route(send, arrive)
        return count[0]

    def z_first(send, arrive):
        zs = [z, z - 1, z + 1, z - 2, z + 2, z - 3, z + 3, z - 4]
        send(me, *(f"z{d}" for d in (1, 7, 2, 6, 3, 5, 4)), "x+", "x-", "s")
        for zz in zs[1:]:
            slot = pb(x, zz, core)
            arrive(slot)
            send(slot, "x+", "x-", "s")
        for i, zz in enumerate(zs):
            slot = pb(x - 1, zz, core)
            arrive(slot)
            send(slot, *(("x+", "s") if i % 2 == 0 else ("s",)))
            slot = pb(x + 1, zz, core)
            arrive(slot)
            send(slot, *(("x-", "s") if i % 2 == 1 else ("s",)))
        for zz in zs:
            slot = pb(x + 2, zz, core)
            arrive(slot)
            send(slot, "s")

    def x_first(send, arrive):
        send(me, "z1", "z7", "x+", "x-", "x2", "s")
        xs = [x, x - 1, x + 1, x + 2]
        for i in range(1, NX):
            slot = pb(xs[i], z, core)
            arrive(slot)
            send(slot, "z1", "z7", "s")
        for dist in range(1, 5):
            for i in range(NX):
                last_plus, last_minus = (4, 3) if i < 2 else (3, 4)
                if dist <= last_plus:
                    slot = pb(xs[i], z - dist, core)
                    arrive(slot)
                    send(slot, *(("z1", "s") if dist < last_plus else ("s",)))
                if dist <= last_minus:
                    slot = pb(xs[i], z + dist, core)
                    arrive(slot)
                    send(slot, *(("z7", "s") if dist < last_minus else ("s",)))

    for o in range(1, NY):
        q_copy(o).start()

    @pl.when(core == 0)
    def _():
        assert run(z_first) == 63

    @pl.when(core == 1)
    def _():
        assert run(x_first) == 63

    for o in range(1, NY):
        q_copy(o).wait()
    queries()

    @pl.loop(0, NX * NZ)
    def _(i):
        copy(2 * i + 1 - core, sibling, 0).wait_recv()
        landed(2 * i + 1 - core)

    def sent():
        @pl.loop(0, 63)
        def _(i):
            copy(me, sibling, i).wait_send()

    return sent


def spread(slot, kbuf, kf_ref):
    for i in range(2):
        base = lax.div(slot, 4) * 512 + (lax.rem(slot, 4) * 2 + i) * 8
        for c in range(CELLS // 8):
            for h in range(2):
                to = pl.multiple_of(base + c * 64, 8) + h * NK
                kf_ref[pl.ds(to, 8), :] = kbuf[slot, i * CELLS + c * 8 : i * CELLS + c * 8 + 8, h * 128 : (h + 1) * 128].astype(f32)


def order_keys(kf_ref, kp_ref):
    @pl.loop(0, CELLS // 4)
    def _(i):
        for u in range(4):
            base = pl.multiple_of(lax.div(i, 2) * 64, 64) + lax.rem(i, 2) * 4 + u
            for h in range(2):
                for t in range(0, NT // 8, 2):
                    pair = [kf_ref[pl.ds(base + (t + j) * 512 + h * NK, 8, stride=8), :] for j in range(2)]
                    rows = pl.ds(pl.multiple_of((i * 4 + (0, 2, 1, 3)[u]) * NT + t * 8, 16), 16)
                    kp_ref[rows, h * 128 : (h + 1) * 128] = jnp.concatenate(pair, axis=0).astype(bf16)


def costs(qall, kp_ref, cost_ref):
    low = lax.broadcasted_iota(jnp.int32, (8, 128), 0) < 4

    @pl.loop(0, CELLS // 16)
    def _(jj):
        for u in range(4):
            j = jj * 4 + u
            r = pl.multiple_of(j * 512, 512)
            even = dot_nt(qall[0], kp_ref[pl.ds(r, 256), :])
            odd = dot_nt(qall[1], kp_ref[pl.ds(r + 256, 256), :])
            for v in range(NQ // 8):
                for h in range(2):
                    ev = even[v * 8 : v * 8 + 8, h * 128 : (h + 1) * 128]
                    od = odd[v * 8 : v * 8 + 8, h * 128 : (h + 1) * 128]
                    to = pl.multiple_of(v * 512 + j * 16 + h * 8, 8)
                    cost_ref[pl.ds(to, 8), :] = jnp.where(low, ev, od)
                    cost_ref[pl.ds(to + 256, 8), :] = jnp.where(low, od, ev)


def pipeline(mask_ref, wd_ref, bias_ref, gain_ref, smap_ref, w_ref, lse_ref, cost_ref, toks, nrms, ps, ms, after):
    lane = lax.broadcasted_iota(jnp.int32, (8, 128), 1)
    sub = lax.broadcasted_iota(jnp.int32, (8, 128), 0)
    lane64 = lax.broadcasted_iota(jnp.int32, (64, 128), 1)

    def sums(g, slot):
        nrm_ref, p_ref, m_ref = nrms[slot], ps[slot], ms[slot]
        b4 = lax.rem(g + 1, 2) * 4
        zero = jnp.zeros((8, 128), f32)
        for hh in range(2):
            rows = []
            for lp in range(LAT):
                st = jnp.bitwise_xor(b4, lp ^ (2 * hh)) + hh * 128
                pa = p_ref[pl.ds(st, 8, stride=8), :]
                pb = p_ref[pl.ds(st + 64, 8, stride=8), :]
                left, right = jnp.concatenate([pa, zero], axis=0), jnp.concatenate([zero, pb], axis=0)
                rows.append(jnp.concatenate([left.astype(bf16), right.astype(bf16)], axis=1))
            lhs = jnp.concatenate([nrm_ref[hh * 512 : hh * 512 + 512, :], jnp.ones((16, 256), bf16)], axis=0)
            o = dot_nt(lhs, jnp.concatenate(rows, axis=0))
            acc = o[0:64, :]
            for p in range(1, 8):
                acc = jnp.where(lax.bitwise_and(lane64, 7) == p, o[p * 64 : (p + 1) * 64, :], acc)
            d = o[512:513, :]
            vl = slice(hh * 128, (hh + 1) * 128)
            w_ref[pl.ds(pl.multiple_of(g * 64, 64), 64), vl] = acc * (1.0 / d)
            lse_ref[pl.ds(pl.multiple_of(g * 8, 8), 8), vl] = jnp.broadcast_to(m_ref[0:1, vl] + jnp.log(d), (8, 128))
            yield

    def scores(g, slot):
        nrm_ref, p_ref, m_ref = nrms[slot], ps[slot], ms[slot]
        b4 = lax.rem(g, 2) * 4
        pos = [lane - jnp.bitwise_xor(sub, b4 + 2 * hh) * 16 for hh in range(2)]
        accm = [jnp.zeros((8, 128), f32)] * 2
        for k in range(NP // 4):
            s3 = jnp.dot(smap_ref[...], nrm_ref[k * 256 : (k + 1) * 256, :], preferred_element_type=f32)
            for i in range(4):
                s = s3[24 * i : 24 * i + 8] + (s3[24 * i + 8 : 24 * i + 16] + s3[24 * i + 16 : 24 * i + 24])
                for h in range(2):
                    hh, p = divmod(k * 4 + i, 8)
                    q = hh * 16 + h * 8 + p
                    sq = s[:, h * 128 : (h + 1) * 128]
                    m = jnp.broadcast_to(jnp.max(sq, axis=1, keepdims=True), (8, 128))
                    p_ref[q * 8 : q * 8 + 8, :] = jnp.exp(sq - m)
                    accm[hh] = jnp.where(pos[hh] == h * 8 + p, m, accm[hh])
            if k < NP // 4 - 1:
                yield
        for hh in range(2):
            m_ref[:, hh * 128 : (hh + 1) * 128] = jnp.broadcast_to(jnp.sum(accm[hh], axis=0, keepdims=True), (8, 128))
        yield

    def norms(slot):
        tok_ref, nrm_ref = toks[slot], nrms[slot]
        for i in range(NP):
            for h in range(2):
                hl = slice(h * 128, (h + 1) * 128)
                tok = tok_ref[i * 64 : (i + 1) * 64, hl] + bias_ref[:, hl]
                ss = jnp.sum(tok * tok, axis=0, keepdims=True)
                rstd = lax.rsqrt(ss * (1.0 / E) + 1e-5)
                nrm_ref[i * 64 : (i + 1) * 64, hl] = (tok * rstd * gain_ref[:, hl]).astype(bf16)
                yield

    def tokens(g, slot):
        q0 = jnp.minimum(g, NG - 1) * G
        for k in range(NP // 2):
            rows = []
            for i in range(2):
                xs = []
                for h in range(2):
                    q = (k * 2 + i) // 8 * 16 + h * 8 + (k * 2 + i) % 8
                    base = pl.multiple_of((q0 + q // 4 * 4) * CELLS, 256) + q % 4
                    xq = cost_ref[pl.ds(base, CELLS, stride=4), :].astype(bf16)
                    mk = jnp.broadcast_to(mask_ref[pl.ds(q0 + q, 1), :].astype(f32), (CELLS, NT)).astype(bf16)
                    xs.append(xq * mk)
                xx = jnp.concatenate(xs, axis=1)
                rows += [xx, xx]
            toks[slot][k * 128 : (k + 1) * 128, :] = jnp.dot(
                wd_ref[k % 4 // 2], jnp.concatenate(rows, axis=0), preferred_element_type=f32
            )
            yield

    def block(g, u, order):
        steps = {"w": sums(g, u), "s": scores(g, (u + 1) % 3), "n": norms((u + 2) % 3), "t": tokens(g, u)}
        for step in order:
            next(steps[step])

    block(0, 0, "t" * 8)
    block(1, 1, "tnnnn" * 8)
    block(2, 2, "snn" * 4 + "tnnn" * 8)

    @pl.loop(1, 7)
    def _(it):
        for u in range(3):
            g = it * 3 + u

            @pl.when(g < NG + 1)
            def _():
                block(g, u, "wnnnnnnnn" * 2 + "snn" * 4 + "tn" * 8)
                after(g)

    block(NG + 1, (NG + 1) % 3, "ww" + "ssss")
    block(NG + 2, (NG + 2) % 3, "ww")
    after(NG + 2)


def split(a, n):
    parts = []
    for _ in range(n):
        parts.append(a.astype(bf16).astype(f32))
        a = a - parts[-1]
    return parts


def parameters(weight_ref, pbias_ref, pgain_ref, latq_ref, key_ref, wd_ref, bias_ref, gain_ref, smap_ref):
    weight = weight_ref[...].astype(f32)
    even = lax.rem(lax.broadcasted_iota(jnp.int32, (CELLS, E), 0), 2) == 0
    swapped = jnp.where(even, pltpu.roll(weight, CELLS - 1, 0), pltpu.roll(weight, 1, 0))
    zero = jnp.zeros((E, 128), f32)
    for i, form in enumerate((weight, swapped)):
        form = form.T
        centred = (form - jnp.mean(form, axis=0, keepdims=True)) / math.sqrt(CH)
        parts = jnp.concatenate(split(centred, 2), axis=1)
        wd_ref[i] = jnp.concatenate(
            [jnp.concatenate([parts, zero], axis=1), jnp.concatenate([zero, parts], axis=1)], axis=0
        ).astype(bf16)
    bias = pbias_ref[...]
    bias = bias - jnp.mean(bias, axis=1, keepdims=True)
    for source, ref in ((bias, bias_ref), (pgain_ref[...], gain_ref)):
        column = jnp.broadcast_to(source, (128, E)).T
        ref[:, 0:128] = column
        ref[:, 128:256] = column
    score_map = lax.dot_general(
        latq_ref[...], key_ref[...].astype(f32), (((1,), (1,)), ((), ())),
        precision=lax.Precision.HIGHEST, preferred_element_type=f32,
    ) / math.sqrt(LD)
    parts = jnp.concatenate(split(score_map, 3), axis=0)
    zero = jnp.zeros_like(parts)
    smap_ref[...] = jnp.concatenate(
        [jnp.concatenate([parts if i == j else zero for j in range(4)], axis=1) for i in range(4)], axis=0
    ).astype(bf16)


def kernel(
    q_ref, k_ref, mask_ref, weight_ref, pbias_ref, pgain_ref, latq_ref, key_ref, value_ref, out_ref,
    kbuf, qbuf, kf_ref, kp_ref, qall, cost_ref, toks, nrms, ps, ms, w_ref, lse_ref, wd_ref, bias_ref, gain_ref, smap_ref,
    sbuf, sst, rbuf, rst, ssem, rsem, qssem, qrsem, dssem, drsem, tssem, trsem,
):
    me = lax.axis_index("pb")
    y = lax.axis_index("ka")
    def prepare():
        parameters(weight_ref, pbias_ref, pgain_ref, latq_ref, key_ref, wd_ref, bias_ref, gain_ref, smap_ref)

    def queries():
        rows = jnp.concatenate([qbuf[i] for i in range(NY)], axis=0).astype(f32).T
        qall[0] = rows.astype(bf16)
        qall[1] = pltpu.roll(rows.reshape(NQ // 8, 8, CH), 4, 1).reshape(NQ, CH).astype(bf16)

    def landed(slot):
        spread(slot, kbuf, kf_ref)

    sent = gather(me, y, k_ref, q_ref, kbuf, qbuf, ssem, rsem, qssem, qrsem, prepare, queries, landed)
    order_keys(kf_ref, kp_ref)
    costs(qall, kp_ref, cost_ref)
    lane64 = lax.broadcasted_iota(jnp.int32, (64, 128), 1)
    lane8 = lax.broadcasted_iota(jnp.int32, (8, 128), 1)

    def copies(k, o):
        to = lax.rem(y + o, NY)
        rows = pl.ds(pl.multiple_of(k * 128, 128), 128)
        st = pl.ds(pl.multiple_of(k * 16, 16), 16)
        return (
            pltpu.make_async_remote_copy(
                src_ref=sbuf.at[to, rows], dst_ref=rbuf.at[o - 1, rows], send_sem=dssem.at[o - 1, k],
                recv_sem=drsem.at[o - 1, k], device_id=(me, to), device_id_type=MESH,
            ),
            pltpu.make_async_remote_copy(
                src_ref=sst.at[to, st], dst_ref=rst.at[o - 1, st], send_sem=tssem.at[o - 1, k],
                recv_sem=trsem.at[o - 1, k], device_id=(me, to), device_id_type=MESH,
            ),
        )

    def quarters(lane, a):
        return jnp.where(lane < 64, jnp.where(lane < 32, a[0], a[1]), jnp.where(lane < 96, a[2], a[3]))

    def send_chunk(k):
        for blk in range(2):
            ga = k * GPC + blk * 2 + 3
            rows = pl.ds(pl.multiple_of(k * 128 + blk * 64, 64), 64)
            st = pl.ds(pl.multiple_of(k * 16 + blk * 8, 8), 8)
            wr = [pl.ds(pl.multiple_of((ga + i) * 64, 64), 64) for i in range(2)]
            lr = [pl.ds(pl.multiple_of((ga + i) * 8, 8), 8) for i in range(2)]
            vl = [slice(hh * 128, (hh + 1) * 128) for hh in range(2)]
            ws = [w_ref[wr[hg // 2], vl[hg % 2]] for hg in range(4)]
            ls = [lse_ref[lr[hg // 2], vl[hg % 2]] for hg in range(4)]
            for j in range(NY):
                sbuf[j, rows, :] = quarters(lane64, [ws[j ^ i] for i in range(4)]).astype(bf16)
                sst[j, st, :] = quarters(lane8, [ls[j ^ i] for i in range(4)])
        for o in range(1, NY):
            for c in copies(k, o):
                c.start()

    def combine_chunk(k):
        for o in range(1, NY):
            for c in copies(k, o):
                c.wait_recv()
        for blk in range(2):
            rows = pl.ds(pl.multiple_of(k * 128 + blk * 64, 64), 64)
            st = pl.ds(pl.multiple_of(k * 16 + blk * 8, 8), 8)
            lses = [sst[y, st, :]] + [rst[o, st, :] for o in range(NY - 1)]
            vals = [sbuf[y, rows, :]] + [rbuf[o, rows, :] for o in range(NY - 1)]
            top = jnp.maximum(jnp.maximum(lses[0], lses[1]), jnp.maximum(lses[2], lses[3]))
            facs = [jnp.exp(a - top) for a in lses]
            inv = 1.0 / (facs[0] + facs[1] + facs[2] + facs[3])
            pooled = sum(v.astype(f32) * (a * inv)[0:1, :] for v, a in zip(vals, facs))
            res = lax.dot_general(
                pooled.astype(bf16), value_ref[...], (((0,), (0,)), ((), ())), preferred_element_type=f32
            ).astype(bf16)
            for i in range(4):
                off = jnp.bitwise_xor(y, i) * 16
                orow = pl.ds(pl.multiple_of(k * 128 + blk * 64 + off, 16), 16)
                for l in range(2):
                    r = i * 32 + l * 16
                    out_ref[orow, l * 128 : (l + 1) * 128] = res[r : r + 16, :]

    def after(g):
        @pl.when(jnp.logical_and(lax.rem(g, GPC) == 2, g > 3))
        def _():
            k = lax.div(g - 3, GPC)
            send_chunk(k)

    pipeline(mask_ref, wd_ref, bias_ref, gain_ref, smap_ref, w_ref, lse_ref, cost_ref, toks, nrms, ps, ms, after)

    def chunk_sent(k):
        for o in range(1, NY):
            for c in copies(k, o):
                c.wait_send()

    sent()
    pl.loop(0, NCH - 1)(chunk_sent)
    pl.loop(0, NCH)(combine_chunk)
    chunk_sent(NCH - 1)


def body(
    query_features, key_features, patch_weight, patch_bias, norm_gain, latent_queries, key_weight, value_weight, keep_mask
):
    vmem = pl.BlockSpec(memory_space=pltpu.VMEM)
    dma = pltpu.SemaphoreType.DMA
    out = pl.pallas_call(
        kernel,
        out_shape=jax.ShapeDtypeStruct((NQ, 2 * LD), bf16),
        in_specs=[vmem] * 9,
        out_specs=vmem,
        scratch_shapes=[
            pltpu.VMEM((2 * NX * NZ, 128, CH), bf16),
            pltpu.VMEM((NY, CH // NY, NQ), bf16),
            pltpu.VMEM((2 * NK, 128), f32),
            pltpu.VMEM((NK, CH), bf16),
            pltpu.VMEM((2, NQ, CH), bf16),
            pltpu.VMEM((CELLS * NQ, NT), f32),
            [pltpu.VMEM((NP * E, 256), f32)] * 3,
            [pltpu.VMEM((NP * E, 256), bf16)] * 3,
            [pltpu.VMEM((G * LAT, NT), f32)] * 3,
            [pltpu.VMEM((8, 256), f32)] * 3,
            pltpu.VMEM(((NG + 3) * E, 256), f32),
            pltpu.VMEM(((NG + 3) * 8, 256), f32),
            pltpu.VMEM((2, 2 * E, 256), bf16),
            pltpu.VMEM((E, 256), f32),
            pltpu.VMEM((E, 256), f32),
            pltpu.VMEM((96, 256), bf16),
            pltpu.VMEM((NY, NQ, 128), bf16),
            pltpu.VMEM((NY, NCH * 16, 128), f32),
            pltpu.VMEM((NY - 1, NQ, 128), bf16),
            pltpu.VMEM((NY - 1, NCH * 16, 128), f32),
            dma((64,)),
            dma((64,)),
            dma((NY - 1,)),
            dma((NY - 1,)),
            dma((NY - 1, NCH)),
            dma((NY - 1, NCH)),
            dma((NY - 1, NCH)),
            dma((NY - 1, NCH)),
        ],
        compiler_params=pltpu.CompilerParams(
            collective_id=0, has_side_effects=True, vmem_limit_bytes=60 * 1024 * 1024
        ),
    )(
        query_features.T, key_features, keep_mask, patch_weight, patch_bias.reshape(1, E), norm_gain.reshape(1, E),
        latent_queries, key_weight, value_weight,
    )
    return out.reshape(NQ, 2, LD)


def solution(mesh):
    placed = (P("pb", "ka"), P(("ka", "pb"), None), P(), P(), P(), P(), P(), P(), P("pb", "ka"))
    return jax.shard_map(
        body, mesh=mesh, in_specs=placed, out_specs=P("pb", "ka", None), check_vma=False
    )
```
